128 devices in a mesh: grp: 64 (over z, y, x), blk: 2 (over core).
Axes of the slice: x: 4, y: 4, z: 4, core: 2. Of those that a mesh axis runs over, the one named last changes fastest.
Arguments:
- embeddings: bfloat16 [131072, 1024], P(('grp', 'blk'))
- labels: int32 [131072], P(('grp', 'blk')), may hold values from 0 to 1023, as said below
- row_ids: int32 [131072], P(('grp', 'blk')), may hold values from 0 to 131071, each once
Outputs:
- best: float32 [131072], P(('grp', 'blk'))
The draws below stay inside these ranges and needn't reach their ends.
Inputs may be any that keep to these rules, and one draw needn't show every extreme that they name: Cluster c is owned by group c divided by 16, rounded down. In each device's aligned block of 1024 rows, at most 32 labels are of clusters that one group owns, and exactly 32 for some group.
All inputs are finite; a program needn't handle non-finite values.
Results may differ from the reference program's by a relative error of at most 0.0006.
Values may be sent and summed in bfloat16 or wider, within the bound.
No kernel may reach another device: no remote copies, remote signals or barrier semaphores. Data moves between devices by JAX's collectives and lax.ppermute only.
A program may use at most 64 MiB of HBM per device.

```python
import math
import jax
import jax.numpy as jnp
from jax import lax

D = 1024
ROWS_DEV = 1024
CAP = 32
CL_GRP = 16
CLUSTERS = 1024
TOTAL = 131072
N_GRP = 64
N_BLK = 2


def cluster_plan(key):
    plan_key = jax.random.fold_in(key, 101)
    groups = CLUSTERS // CL_GRP
    devices = TOTAL // ROWS_DEV
    common = jax.random.randint(jax.random.fold_in(plan_key, 2), (1, 1), 0, groups)
    busy = jnp.broadcast_to(common, (devices, 1))
    remaining = ROWS_DEV - CAP
    full_count = remaining // (2 * CAP)
    spread_count = groups - 1 - full_count
    orders = jax.vmap(lambda k: jax.random.permutation(k, groups - 1))(jax.random.split(jax.random.fold_in(plan_key, 5), devices)).astype(jnp.int32)
    place = jnp.arange(ROWS_DEV, dtype=jnp.int32)[None, :]
    tail = place - CAP
    choice_col = jnp.where(tail < full_count * CAP, tail // CAP, full_count + (tail - full_count * CAP) % spread_count)
    choice_col = jnp.clip(choice_col, 0, groups - 2).astype(jnp.int32)
    choice_col = jnp.broadcast_to(choice_col, (devices, ROWS_DEV))
    offsets = jnp.take_along_axis(orders, choice_col, axis=1)
    target = jnp.where(place < CAP, busy, (busy + 1 + offsets) % groups)
    shuffles = jax.vmap(lambda k: jax.random.permutation(k, ROWS_DEV))(jax.random.split(jax.random.fold_in(plan_key, 3), devices))
    target = jnp.take_along_axis(target, shuffles.astype(jnp.int32), axis=1)
    choose = jax.random.randint(jax.random.fold_in(plan_key, 4), (devices, ROWS_DEV), 0, CL_GRP)
    within = choose * choose // CL_GRP
    return (target * CL_GRP + within).reshape(TOTAL).astype(jnp.int32)


def draw_labels(key, part):
    return cluster_plan(key)


def draw_embeddings(key, part):
    labels = cluster_plan(key)
    key = jax.random.fold_in(key, 7)
    centers = jax.random.normal(jax.random.fold_in(key, 1), (CLUSTERS, D), jnp.float32)
    subcenters = jax.random.normal(jax.random.fold_in(key, 5), (CLUSTERS, 2, D), jnp.float32)
    side = jax.random.randint(jax.random.fold_in(key, 4), (TOTAL,), 0, 2).astype(jnp.int32)
    anchor = centers[labels] + subcenters[labels, side]
    spread = jnp.exp(jax.random.uniform(jax.random.fold_in(key, 2), (TOTAL, 1), jnp.float32, jnp.log(0.1), jnp.log(3.0)))
    noise = jax.random.normal(jax.random.fold_in(key, 3), (TOTAL, D), jnp.float32)
    return (spread * anchor + noise).astype(jnp.bfloat16)


def setup_inputs(seed: int = 0) -> dict:
    keys = jax.random.split(jax.random.key(seed), 4)
    return {
        "embeddings": draw_embeddings(jax.random.fold_in(keys[3], 71), 0),
        "labels": draw_labels(jax.random.fold_in(keys[3], 71), 0),
        "row_ids": jax.random.permutation(keys[2], TOTAL).astype(jnp.int32),
    }


def reference(embeddings, labels, row_ids):
    wide = embeddings.astype(jnp.float32)
    unit = (wide * lax.rsqrt(lax.optimization_barrier(jnp.sum(wide * wide, axis=1, keepdims=True)) + 1e-06)).astype(jnp.bfloat16)
    group_of = (labels // CL_GRP).astype(jnp.int32)
    keys_all = CAP * N_GRP * N_BLK
    qblock = math.gcd(512, keys_all)

    def one_group(grp_index, result):
        member = group_of == grp_index
        picked = jnp.nonzero(member, size=keys_all, fill_value=0)[0].astype(jnp.int32)
        count = jnp.sum(member.astype(jnp.int32))
        valid = jnp.arange(keys_all, dtype=jnp.int32) < count
        vectors = unit[picked]
        key_lab = jnp.where(valid, labels[picked], -1)
        key_ids = row_ids[picked]

        def rows_block(block):
            qvec, qlab, qids = block
            gram = jnp.dot(qvec, vectors.T, preferred_element_type=jnp.float32)
            mask = (key_lab[None, :] == qlab[:, None]) & (key_ids[None, :] < qids[:, None]) & (key_lab[None, :] >= 0)
            return lax.optimization_barrier(jnp.max(jnp.where(mask, gram, jnp.float32(-1.0)), axis=1))
        found = lax.map(rows_block, (vectors.reshape(keys_all // qblock, qblock, -1), key_lab.reshape(keys_all // qblock, qblock), key_ids.reshape(keys_all // qblock, qblock))).reshape(keys_all)
        target = jnp.where(valid, picked, TOTAL).astype(jnp.int32)
        return result.at[target].set(found, mode='drop')
    start = jnp.full((TOTAL,), -1.0, jnp.float32)
    return lax.fori_loop(0, N_GRP, one_group, start)
```

```python
import functools

import jax
import jax.numpy as jnp
from jax import lax
from jax.experimental import pallas as pl
from jax.experimental.pallas import tpu as pltpu
from jax.sharding import PartitionSpec as P

CAP = 32
CL_GRP = 16
LANES = 128
NT = (((1,), (1,)), ((), ()))


def pack_kernel(groups, labels_ref, ids_ref, emb_ref, out_ref, slot_ref, raw, unit, slots, meta, sems):
    step = pl.program_id(0)
    block = out_ref.shape[0]
    rows, width = unit.shape
    lines = rows // LANES
    parts = sems.shape[0]
    part = rows // parts

    def copy(p):
        span = pl.ds(p * part, part)
        return pltpu.make_async_copy(emb_ref.at[span], raw.at[span], sems.at[p])

    @pl.when(step == 0)
    def _():
        for p in range(parts):
            copy(p).start()
        labels = labels_ref[...]
        place = (
            lax.broadcasted_iota(jnp.int32, (lines, LANES), 0) * LANES
            + lax.broadcasted_iota(jnp.int32, (lines, LANES), 1)
        )
        key = (labels * rows + place).astype(jnp.float32)
        target = lax.shift_right_logical(labels, 4)
        low = (target * (CL_GRP * rows)).astype(jnp.float32)
        tall = jnp.concatenate([key, jnp.zeros((LANES - lines, LANES), jnp.float32)], axis=0).T

        def flat(x):
            return jnp.concatenate([x[b : b + 1] for b in range(lines)], axis=1)

        key_row, low_row = flat(key), flat(low)
        count = jnp.zeros((LANES, rows), jnp.float32)
        for b in range(lines):
            col = tall[:, b : b + 1]
            count += jnp.where((col >= low_row) & (col < key_row), 1.0, 0.0)
        rank = jnp.sum(count, axis=0, keepdims=True)
        slot = flat(target * CAP) + rank.astype(jnp.int32)
        slots[...] = slot
        slot_ref[...] = slot
        ids = ids_ref[...]
        first = flat((ids & 255).astype(jnp.float32))
        second = flat((lax.shift_right_logical(ids, 8) & 255).astype(jnp.float32))
        third = flat(
            ((labels & (CL_GRP - 1)) * 2 + lax.shift_right_logical(ids, 16) + 1).astype(jnp.float32)
        )
        meta[...] = jnp.concatenate(
            [first, second, third, jnp.zeros((meta.shape[0] - 3, rows), jnp.float32)], axis=0
        ).astype(jnp.bfloat16)
        for p in range(parts):
            copy(p).wait()
            wide = raw[p * part : (p + 1) * part].astype(jnp.float32)
            scale = lax.rsqrt(jnp.sum(wide * wide, axis=1, keepdims=True) + 1e-06)
            unit[p * part : (p + 1) * part] = (wide * scale).astype(jnp.bfloat16)

    span = block * CAP
    base = step * span
    wanted = lax.broadcasted_iota(jnp.int32, (span, rows), 0) + base
    pick = jnp.where(slots[...] == wanted, 1.0, 0.0).astype(jnp.bfloat16)
    packed = jnp.dot(pick, unit[...], preferred_element_type=jnp.float32).astype(jnp.bfloat16)
    for j in range(width // LANES):
        out_ref[:, j * CAP : (j + 1) * CAP, :] = packed[:, j * LANES : (j + 1) * LANES].reshape(
            block, CAP, LANES
        )
    tags = lax.dot_general(meta[...], pick, NT, preferred_element_type=jnp.float32)
    tail = width // LANES * CAP
    for g in range(block):
        at = g * CAP // LANES * LANES
        line = tags[:8, at : at + LANES]
        turn = g * CAP % LANES
        if turn:
            line = pltpu.roll(line, LANES - turn, 1)
        out_ref[g, tail : tail + 8, :] = line.astype(jnp.bfloat16)


def pack(embeddings, labels, row_ids, groups):
    rows, width = embeddings.shape
    lines = rows // LANES
    depth = width // LANES * CAP + 8
    block = 16
    parts = 4
    return pl.pallas_call(
        functools.partial(pack_kernel, groups),
        grid=(groups // block,),
        in_specs=[
            pl.BlockSpec((lines, LANES), lambda i: (0, 0)),
            pl.BlockSpec((lines, LANES), lambda i: (0, 0)),
            pl.BlockSpec(memory_space=pl.ANY),
        ],
        out_specs=[
            pl.BlockSpec((block, depth, LANES), lambda i: (i, 0, 0)),
            pl.BlockSpec((1, rows), lambda i: (0, 0)),
        ],
        out_shape=[
            jax.ShapeDtypeStruct((groups, depth, LANES), jnp.bfloat16),
            jax.ShapeDtypeStruct((1, rows), jnp.int32),
        ],
        scratch_shapes=[
            pltpu.VMEM((rows, width), jnp.bfloat16),
            pltpu.VMEM((rows, width), jnp.bfloat16),
            pltpu.VMEM((1, rows), jnp.int32),
            pltpu.VMEM((16, rows), jnp.bfloat16),
            pltpu.SemaphoreType.DMA((parts,)),
        ],
        compiler_params=pltpu.CompilerParams(vmem_limit_bytes=48 << 20),
        cost_estimate=pl.CostEstimate(
            flops=2 * groups * CAP * rows * width, bytes_accessed=6 * rows * width, transcendentals=rows
        ),
    )(labels.reshape(lines, LANES), row_ids.reshape(lines, LANES), embeddings)


def codes(block):
    tags = block.astype(jnp.float32)
    return (tags[:, 2, :] - 1.0) * 65536.0 + tags[:, 1, :] * 256.0 + tags[:, 0, :]


def gram_kernel(q_ref, k_ref, prev_ref, out_ref, vecs, order, q_code, q_low, acc):
    step = pl.program_id(0)
    senders = q_ref.shape[0]
    chunks = vecs.shape[1] // LANES
    tail = chunks * CAP
    block = k_ref.shape[0]
    per = LANES // CAP
    lines = senders // per
    lane = lax.broadcasted_iota(jnp.int32, (lines, LANES), 1)

    @pl.when(step == 0)
    def _():
        for j in range(chunks):
            vecs[:, j * LANES : (j + 1) * LANES] = q_ref[:, j * CAP : (j + 1) * CAP, :].reshape(
                senders * CAP, LANES
            )
        order[...] = codes(q_ref[:, tail : tail + 8, :])
        code = order[pl.ds(0, lines, stride=per), :]
        for k in range(1, per):
            code = jnp.where(
                lane >= k * CAP, pltpu.roll(order[pl.ds(k, lines, stride=per), :], k * CAP, 1), code
            )
        low = jnp.floor(code * (1.0 / 131072.0)) * 131072.0
        for t in range(lines):
            q_code[:, t * LANES : (t + 1) * LANES] = code[t : t + 1]
            q_low[:, t * LANES : (t + 1) * LANES] = low[t : t + 1]
        acc[...] = jnp.full(acc.shape, -1.0, jnp.float32)

    keys = jnp.concatenate(
        [
            k_ref[:, j * CAP : (j + 1) * CAP, :].reshape(block * CAP, LANES)
            for j in range(chunks)
        ],
        axis=1,
    )
    k_code = codes(k_ref[:, tail : tail + 8, :])
    tall = jnp.concatenate([k_code, jnp.zeros((LANES - block, LANES), jnp.float32)], axis=0).T
    col = jnp.concatenate([tall[:CAP, s : s + 1] for s in range(block)], axis=0)
    wide = 512
    for c in range(senders * CAP // wide):
        span = slice(c * wide, (c + 1) * wide)
        score = lax.dot_general(keys, vecs[span], NT, preferred_element_type=jnp.float32)
        seen = (col >= q_low[:, span]) & (col < q_code[:, span])
        score = jnp.where(seen, score, -1.0)
        acc[:, span] = jnp.maximum(
            acc[:, span], jnp.max(score.reshape(block * CAP // 8, 8, wide), axis=0)
        )

    @pl.when(step == pl.num_programs(0) - 1)
    def _():
        best = jnp.max(acc[...], axis=0, keepdims=True)
        best = jnp.concatenate([best[:, t * LANES : (t + 1) * LANES] for t in range(lines)], axis=0)
        for k in range(per):
            turned = pltpu.roll(best, LANES - k * CAP, 1) if k else best
            order[pl.ds(k, lines, stride=per), :] = turned
        out_ref[...] = jnp.maximum(prev_ref[...], order[...])


def gram(queries, keys, prev):
    senders, depth, _ = queries.shape
    chunks = depth // CAP
    block = 8
    count = senders * CAP
    return pl.pallas_call(
        gram_kernel,
        grid=(senders // block,),
        in_specs=[
            pl.BlockSpec((senders, depth, LANES), lambda i: (0, 0, 0)),
            pl.BlockSpec((block, depth, LANES), lambda i: (i, 0, 0)),
            pl.BlockSpec((senders, LANES), lambda i: (0, 0)),
        ],
        out_specs=pl.BlockSpec((senders, LANES), lambda i: (0, 0)),
        out_shape=jax.ShapeDtypeStruct((senders, LANES), jnp.float32),
        scratch_shapes=[
            pltpu.VMEM((count, chunks * LANES), jnp.bfloat16),
            pltpu.VMEM((senders, LANES), jnp.float32),
            pltpu.VMEM((1, count), jnp.float32),
            pltpu.VMEM((1, count), jnp.float32),
            pltpu.VMEM((8, count), jnp.float32),
        ],
        compiler_params=pltpu.CompilerParams(vmem_limit_bytes=48 << 20),
        cost_estimate=pl.CostEstimate(
            flops=2 * count * count * chunks * LANES,
            bytes_accessed=4 * count * chunks * LANES,
            transcendentals=0,
        ),
    )(queries, keys, prev)


def unpack_kernel(back_ref, slot_ref, out_ref):
    groups = back_ref.shape[0]
    rows = slot_ref.shape[1]
    slot = slot_ref[...]
    group = lax.shift_right_logical(slot, 5)
    rank = slot & (CAP - 1)
    member = lax.broadcasted_iota(jnp.int32, (groups, rows), 0) == group
    member = jnp.where(member, 1.0, 0.0).astype(jnp.bfloat16)
    rest = back_ref[...]
    found = jnp.zeros((LANES, rows), jnp.float32)
    for _ in range(3):
        piece = rest.astype(jnp.bfloat16)
        rest = rest - piece.astype(jnp.float32)
        found += lax.dot_general(
            piece, member, (((0,), (0,)), ((), ())), preferred_element_type=jnp.float32
        )
    chosen = lax.broadcasted_iota(jnp.int32, (CAP, rows), 0) == rank
    best = jnp.sum(jnp.where(chosen, found[:CAP], 0.0), axis=0, keepdims=True)
    out_ref[...] = jnp.concatenate(
        [best[:, b * LANES : (b + 1) * LANES] for b in range(rows // LANES)], axis=0
    )


def unpack(back, slot):
    rows = slot.shape[1]
    return pl.pallas_call(
        unpack_kernel,
        out_shape=jax.ShapeDtypeStruct((rows // LANES, LANES), jnp.float32),
    )(back, slot)


def local(embeddings, labels, row_ids):
    groups = lax.axis_size("grp")
    rows = embeddings.shape[0]
    send, slot = pack(embeddings, labels, row_ids, groups)
    own = lax.all_to_all(send, "grp", split_axis=0, concat_axis=0, tiled=True)
    other = lax.ppermute(own, "blk", [(0, 1), (1, 0)])
    found = jnp.full((groups, LANES), -1.0, jnp.float32)
    found = gram(own, own, found)
    found = gram(own, other, found)
    back = lax.all_to_all(found, "grp", split_axis=0, concat_axis=0, tiled=True)
    return unpack(back, slot).reshape(rows)


def solution(mesh):
    in_specs = (P(("grp", "blk"), None), P(("grp", "blk")), P(("grp", "blk")))
    out_specs = P(("grp", "blk"))
    return jax.shard_map(local, mesh=mesh, in_specs=in_specs, out_specs=out_specs, check_vma=False)
```

```python
import functools

import jax
import jax.numpy as jnp
from jax import lax
from jax.experimental import pallas as pl
from jax.experimental.pallas import tpu as pltpu
from jax.sharding import PartitionSpec as P

CAP = 32
CL_GRP = 16
LANES = 128
NT = (((1,), (1,)), ((), ()))


def pack_kernel(groups, labels_ref, ids_ref, emb_ref, out_ref, slot_ref, raw, unit, slots, meta, sems):
    step = pl.program_id(0)
    block = out_ref.shape[0]
    rows, width = unit.shape
    lines = rows // LANES
    parts = sems.shape[0]
    part = rows // parts

    def copy(p):
        span = pl.ds(p * part, part)
        return pltpu.make_async_copy(emb_ref.at[span], raw.at[span], sems.at[p])

    @pl.when(step == 0)
    def _():
        for p in range(parts):
            copy(p).start()
        labels = labels_ref[...]
        place = (
            lax.broadcasted_iota(jnp.int32, (lines, LANES), 0) * LANES
            + lax.broadcasted_iota(jnp.int32, (lines, LANES), 1)
        )
        key = (labels * rows + place).astype(jnp.float32)
        target = lax.shift_right_logical(labels, 4)
        low = (target * (CL_GRP * rows)).astype(jnp.float32)
        tall = jnp.concatenate([key, jnp.zeros((LANES - lines, LANES), jnp.float32)], axis=0).T

        def flat(x):
            return jnp.concatenate([x[b : b + 1] for b in range(lines)], axis=1)

        key_row, low_row = flat(key), flat(low)
        count = jnp.zeros((LANES, rows), jnp.float32)
        for b in range(lines):
            col = tall[:, b : b + 1]
            count += jnp.where((col >= low_row) & (col < key_row), 1.0, 0.0)
        rank = jnp.sum(count, axis=0, keepdims=True)
        slot = flat(target * CAP) + rank.astype(jnp.int32)
        slots[...] = slot
        slot_ref[...] = slot
        ids = ids_ref[...]
        first = flat((ids & 255).astype(jnp.float32))
        second = flat((lax.shift_right_logical(ids, 8) & 255).astype(jnp.float32))
        third = flat(
            ((labels & (CL_GRP - 1)) * 2 + lax.shift_right_logical(ids, 16) + 1).astype(jnp.float32)
        )
        meta[...] = jnp.concatenate(
            [first, second, third, jnp.zeros((meta.shape[0] - 3, rows), jnp.float32)], axis=0
        ).astype(jnp.bfloat16)
        for p in range(parts):
            copy(p).wait()
            wide = raw[p * part : (p + 1) * part].astype(jnp.float32)
            scale = lax.rsqrt(jnp.sum(wide * wide, axis=1, keepdims=True) + 1e-06)
            unit[p * part : (p + 1) * part] = (wide * scale).astype(jnp.bfloat16)

    span = block * CAP
    base = step * span
    wanted = lax.broadcasted_iota(jnp.int32, (span, rows), 0) + base
    pick = jnp.where(slots[...] == wanted, 1.0, 0.0).astype(jnp.bfloat16)
    packed = jnp.dot(pick, unit[...], preferred_element_type=jnp.float32).astype(jnp.bfloat16)
    for j in range(width // LANES):
        out_ref[:, j * CAP : (j + 1) * CAP, :] = packed[:, j * LANES : (j + 1) * LANES].reshape(
            block, CAP, LANES
        )
    tags = lax.dot_general(meta[...], pick, NT, preferred_element_type=jnp.float32)
    tail = width // LANES * CAP
    for g in range(block):
        at = g * CAP // LANES * LANES
        line = tags[:8, at : at + LANES]
        turn = g * CAP % LANES
        if turn:
            line = pltpu.roll(line, LANES - turn, 1)
        out_ref[g, tail : tail + 8, :] = line.astype(jnp.bfloat16)


def pack(embeddings, labels, row_ids, groups):
    rows, width = embeddings.shape
    lines = rows // LANES
    depth = width // LANES * CAP + 8
    block = 16
    parts = 4
    return pl.pallas_call(
        functools.partial(pack_kernel, groups),
        grid=(groups // block,),
        in_specs=[
            pl.BlockSpec((lines, LANES), lambda i: (0, 0)),
            pl.BlockSpec((lines, LANES), lambda i: (0, 0)),
            pl.BlockSpec(memory_space=pl.ANY),
        ],
        out_specs=[
            pl.BlockSpec((block, depth, LANES), lambda i: (i, 0, 0)),
            pl.BlockSpec((1, rows), lambda i: (0, 0)),
        ],
        out_shape=[
            jax.ShapeDtypeStruct((groups, depth, LANES), jnp.bfloat16),
            jax.ShapeDtypeStruct((1, rows), jnp.int32),
        ],
        scratch_shapes=[
            pltpu.VMEM((rows, width), jnp.bfloat16),
            pltpu.VMEM((rows, width), jnp.bfloat16),
            pltpu.VMEM((1, rows), jnp.int32),
            pltpu.VMEM((16, rows), jnp.bfloat16),
            pltpu.SemaphoreType.DMA((parts,)),
        ],
        compiler_params=pltpu.CompilerParams(vmem_limit_bytes=62 << 20),
        cost_estimate=pl.CostEstimate(
            flops=2 * groups * CAP * rows * width, bytes_accessed=6 * rows * width, transcendentals=rows
        ),
    )(labels.reshape(lines, LANES), row_ids.reshape(lines, LANES), embeddings)


def codes(block):
    tags = block.astype(jnp.float32)
    return (tags[:, 2, :] - 1.0) * 65536.0 + tags[:, 1, :] * 256.0 + tags[:, 0, :]


def rows_of(ref, sender, count):
    chunks = ref.shape[1] // CAP
    return jnp.concatenate(
        [
            ref[sender : sender + count, j * CAP : (j + 1) * CAP, :].reshape(count * CAP, LANES)
            for j in range(chunks)
        ],
        axis=1,
    )


def gram_kernel(q_ref, k_ref, prev_ref, out_ref, order, q_code, q_low, k_code, acc, *scores):
    senders, depth, _ = q_ref.shape
    tail = depth // CAP * CAP
    per = LANES // CAP
    lines = senders // per
    lane = lax.broadcasted_iota(jnp.int32, (lines, LANES), 1)
    order[...] = codes(q_ref[:, tail : tail + 8, :])
    code = order[pl.ds(0, lines, stride=per), :]
    for k in range(1, per):
        code = jnp.where(
            lane >= k * CAP, pltpu.roll(order[pl.ds(k, lines, stride=per), :], k * CAP, 1), code
        )
    low = jnp.floor(code * (1.0 / 131072.0)) * 131072.0
    for t in range(lines):
        q_code[:, t * LANES : (t + 1) * LANES] = code[t : t + 1]
        q_low[:, t * LANES : (t + 1) * LANES] = low[t : t + 1]
    tall = codes(k_ref[:, tail : tail + 8, :])
    tall = jnp.concatenate([tall, jnp.zeros((LANES - senders, LANES), jnp.float32)], axis=0).T
    for s in range(senders):
        k_code[s * CAP : (s + 1) * CAP, :] = jnp.broadcast_to(tall[:CAP, s : s + 1], (CAP, LANES))
    acc[...] = jnp.full(acc.shape, -1.0, jnp.float32)

    def reduce_tile(at, k0, q0):
        score = scores[at]
        size, wide = score.shape
        for c in range(0, wide, LANES):
            span = slice(q0 + c, q0 + c + LANES)
            col = k_code[k0 : k0 + size, :]
            seen = (col >= q_low[:, span]) & (col < q_code[:, span])
            part = jnp.where(seen, score[:, c : c + LANES], -1.0).reshape(size // 8, 8, LANES)
            acc[:, span] = jnp.maximum(acc[:, span], jnp.max(part, axis=0))

    size, wide = scores[0].shape
    tiles = [(k0, q0) for k0 in range(0, senders * CAP, size) for q0 in range(0, senders * CAP, wide)]
    for n, (k0, q0) in enumerate(tiles):
        scores[n % 2][...] = lax.dot_general(
            rows_of(k_ref, k0 // CAP, size // CAP),
            rows_of(q_ref, q0 // CAP, wide // CAP),
            NT,
            preferred_element_type=jnp.float32,
        )
        if n:
            reduce_tile((n - 1) % 2, *tiles[n - 1])
    reduce_tile((len(tiles) - 1) % 2, *tiles[-1])

    best = jnp.max(acc[...], axis=0, keepdims=True)
    best = jnp.concatenate([best[:, t * LANES : (t + 1) * LANES] for t in range(lines)], axis=0)
    for k in range(per):
        order[pl.ds(k, lines, stride=per), :] = pltpu.roll(best, LANES - k * CAP, 1) if k else best
    out_ref[...] = jnp.maximum(prev_ref[...], order[...])


def gram(queries, keys, prev):
    senders, depth, _ = queries.shape
    chunks = depth // CAP
    count = senders * CAP
    tile = min(1024, count)
    here = pl.BlockSpec(memory_space=pltpu.VMEM)
    return pl.pallas_call(
        gram_kernel,
        in_specs=[here] * 3,
        out_specs=here,
        out_shape=jax.ShapeDtypeStruct((senders, LANES), jnp.float32),
        scratch_shapes=[
            pltpu.VMEM((senders, LANES), jnp.float32),
            pltpu.VMEM((1, count), jnp.float32),
            pltpu.VMEM((1, count), jnp.float32),
            pltpu.VMEM((count, LANES), jnp.float32),
            pltpu.VMEM((8, count), jnp.float32),
            pltpu.VMEM((tile, tile), jnp.float32),
            pltpu.VMEM((tile, tile), jnp.float32),
        ],
        compiler_params=pltpu.CompilerParams(vmem_limit_bytes=24 << 20),
        cost_estimate=pl.CostEstimate(
            flops=2 * count * count * chunks * LANES,
            bytes_accessed=4 * count * chunks * LANES,
            transcendentals=0,
        ),
    )(queries, keys, prev)


def unpack_kernel(back_ref, slot_ref, out_ref):
    groups = back_ref.shape[0]
    rows = slot_ref.shape[1]
    slot = slot_ref[...]
    group = lax.shift_right_logical(slot, 5)
    rank = slot & (CAP - 1)
    member = lax.broadcasted_iota(jnp.int32, (groups, rows), 0) == group
    member = jnp.where(member, 1.0, 0.0).astype(jnp.bfloat16)
    rest = back_ref[...]
    found = jnp.zeros((LANES, rows), jnp.float32)
    for _ in range(3):
        piece = rest.astype(jnp.bfloat16)
        rest = rest - piece.astype(jnp.float32)
        found += lax.dot_general(
            piece, member, (((0,), (0,)), ((), ())), preferred_element_type=jnp.float32
        )
    chosen = lax.broadcasted_iota(jnp.int32, (CAP, rows), 0) == rank
    best = jnp.sum(jnp.where(chosen, found[:CAP], 0.0), axis=0, keepdims=True)
    out_ref[...] = jnp.concatenate(
        [best[:, b * LANES : (b + 1) * LANES] for b in range(rows // LANES)], axis=0
    )


def unpack(back, slot):
    rows = slot.shape[1]
    return pl.pallas_call(
        unpack_kernel,
        out_shape=jax.ShapeDtypeStruct((rows // LANES, LANES), jnp.float32),
    )(back, slot)


def local(embeddings, labels, row_ids):
    groups = lax.axis_size("grp")
    rows = embeddings.shape[0]
    send, slot = pack(embeddings, labels, row_ids, groups)
    own = lax.all_to_all(send, "grp", split_axis=0, concat_axis=0, tiled=True)
    other = lax.ppermute(own, "blk", [(0, 1), (1, 0)])
    found = jnp.full((groups, LANES), -1.0, jnp.float32)
    found = gram(own, own, found)
    found = gram(own, other, found)
    back = lax.all_to_all(found, "grp", split_axis=0, concat_axis=0, tiled=True)
    return unpack(back, slot).reshape(rows)


def solution(mesh):
    in_specs = (P(("grp", "blk"), None), P(("grp", "blk")), P(("grp", "blk")))
    out_specs = P(("grp", "blk"))
    return jax.shard_map(local, mesh=mesh, in_specs=in_specs, out_specs=out_specs, check_vma=False)
```

```python
import functools

import jax
import jax.numpy as jnp
from jax import lax
from jax.experimental import pallas as pl
from jax.experimental.pallas import tpu as pltpu
from jax.sharding import PartitionSpec as P

CAP = 32
CL_GRP = 16
LANES = 128
NT = (((1,), (1,)), ((), ()))


def pack_kernel(groups, labels_ref, ids_ref, emb_ref, out_ref, slot_ref, raw, unit, slots, meta, sems):
    step = pl.program_id(0)
    block = out_ref.shape[0]
    rows, width = unit.shape
    lines = rows // LANES
    parts = sems.shape[0]
    part = rows // parts

    def copy(p):
        span = pl.ds(p * part, part)
        return pltpu.make_async_copy(emb_ref.at[span], raw.at[span], sems.at[p])

    @pl.when(step == 0)
    def _():
        for p in range(parts):
            copy(p).start()
        labels = labels_ref[...]
        place = (
            lax.broadcasted_iota(jnp.int32, (lines, LANES), 0) * LANES
            + lax.broadcasted_iota(jnp.int32, (lines, LANES), 1)
        )
        key = (labels * rows + place).astype(jnp.float32)
        target = lax.shift_right_logical(labels, 4)
        low = (target * (CL_GRP * rows)).astype(jnp.float32)
        tall = jnp.concatenate([key, jnp.zeros((LANES - lines, LANES), jnp.float32)], axis=0).T

        def flat(x):
            return jnp.concatenate([x[b : b + 1] for b in range(lines)], axis=1)

        key_row, low_row = flat(key), flat(low)
        count = jnp.zeros((LANES, rows), jnp.float32)
        for b in range(lines):
            col = tall[:, b : b + 1]
            count += jnp.where((col >= low_row) & (col < key_row), 1.0, 0.0)
        rank = jnp.sum(count, axis=0, keepdims=True)
        slot = flat(target * CAP) + rank.astype(jnp.int32)
        slots[...] = slot
        slot_ref[...] = slot
        ids = ids_ref[...]
        first = flat((ids & 255).astype(jnp.float32))
        second = flat((lax.shift_right_logical(ids, 8) & 255).astype(jnp.float32))
        third = flat(
            ((labels & (CL_GRP - 1)) * 2 + lax.shift_right_logical(ids, 16) + 1).astype(jnp.float32)
        )
        meta[...] = jnp.concatenate(
            [first, second, third, jnp.zeros((meta.shape[0] - 3, rows), jnp.float32)], axis=0
        ).astype(jnp.bfloat16)
        for p in range(parts):
            copy(p).wait()
            wide = raw[p * part : (p + 1) * part].astype(jnp.float32)
            scale = lax.rsqrt(jnp.sum(wide * wide, axis=1, keepdims=True) + 1e-06)
            unit[p * part : (p + 1) * part] = (wide * scale).astype(jnp.bfloat16)

    span = block * CAP
    base = step * span
    wanted = lax.broadcasted_iota(jnp.int32, (span, rows), 0) + base
    pick = jnp.where(slots[...] == wanted, 1.0, 0.0).astype(jnp.bfloat16)
    packed = jnp.dot(pick, unit[...], preferred_element_type=jnp.float32).astype(jnp.bfloat16)
    for j in range(width // LANES):
        out_ref[:, j * CAP : (j + 1) * CAP, :] = packed[:, j * LANES : (j + 1) * LANES].reshape(
            block, CAP, LANES
        )
    tags = lax.dot_general(meta[...], pick, NT, preferred_element_type=jnp.float32)
    tail = width // LANES * CAP
    for g in range(block):
        at = g * CAP // LANES * LANES
        line = tags[:8, at : at + LANES]
        turn = g * CAP % LANES
        if turn:
            line = pltpu.roll(line, LANES - turn, 1)
        out_ref[g, tail : tail + 8, :] = line.astype(jnp.bfloat16)


def pack(embeddings, labels, row_ids, groups):
    rows, width = embeddings.shape
    lines = rows // LANES
    depth = width // LANES * CAP + 8
    block = 16
    parts = 4
    return pl.pallas_call(
        functools.partial(pack_kernel, groups),
        grid=(groups // block,),
        in_specs=[
            pl.BlockSpec((lines, LANES), lambda i: (0, 0)),
            pl.BlockSpec((lines, LANES), lambda i: (0, 0)),
            pl.BlockSpec(memory_space=pl.ANY),
        ],
        out_specs=[
            pl.BlockSpec((block, depth, LANES), lambda i: (i, 0, 0)),
            pl.BlockSpec((1, rows), lambda i: (0, 0)),
        ],
        out_shape=[
            jax.ShapeDtypeStruct((groups, depth, LANES), jnp.bfloat16),
            jax.ShapeDtypeStruct((1, rows), jnp.int32),
        ],
        scratch_shapes=[
            pltpu.VMEM((rows, width), jnp.bfloat16),
            pltpu.VMEM((rows, width), jnp.bfloat16),
            pltpu.VMEM((1, rows), jnp.int32),
            pltpu.VMEM((16, rows), jnp.bfloat16),
            pltpu.SemaphoreType.DMA((parts,)),
        ],
        compiler_params=pltpu.CompilerParams(vmem_limit_bytes=62 << 20),
        cost_estimate=pl.CostEstimate(
            flops=2 * groups * CAP * rows * width, bytes_accessed=6 * rows * width, transcendentals=rows
        ),
    )(labels.reshape(lines, LANES), row_ids.reshape(lines, LANES), embeddings)


def codes(block):
    tags = block.astype(jnp.float32)
    return (tags[:, 2, :] - 1.0) * 65536.0 + tags[:, 1, :] * 256.0 + tags[:, 0, :]


def low_of(code):
    return jnp.floor(code * (1.0 / 131072.0)) * 131072.0


def code_lines(ref, order):
    senders, depth, _ = ref.shape
    tail = depth // CAP * CAP
    per = LANES // CAP
    lines = senders // per
    lane = lax.broadcasted_iota(jnp.int32, (lines, LANES), 1)
    order[...] = codes(ref[:, tail : tail + 8, :])
    code = order[pl.ds(0, lines, stride=per), :]
    for k in range(1, per):
        turned = pltpu.roll(order[pl.ds(k, lines, stride=per), :], k * CAP, 1)
        code = jnp.where(lane >= k * CAP, turned, code)
    return code


def code_columns(ref, col_code, col_low):
    senders, depth, _ = ref.shape
    tail = depth // CAP * CAP
    tall = codes(ref[:, tail : tail + 8, :])
    tall = jnp.concatenate([tall, jnp.zeros((LANES - senders, LANES), jnp.float32)], axis=0).T
    for s in range(senders):
        col = jnp.broadcast_to(tall[:CAP, s : s + 1], (CAP, LANES))
        col_code[s * CAP : (s + 1) * CAP, :] = col
        col_low[s * CAP : (s + 1) * CAP, :] = low_of(col)


def rows_of(ref, sender, count):
    chunks = ref.shape[1] // CAP
    return jnp.concatenate(
        [
            ref[pl.ds(sender, count), j * CAP : (j + 1) * CAP, :].reshape(count * CAP, LANES)
            for j in range(chunks)
        ],
        axis=1,
    )


def reduce_tile(score, wide, row0, col_code, col_low, col_best, lanes):
    size = score.shape[0]
    step = 64
    tops = [None] * (wide // LANES)
    for r in range(0, size, step):
        rows = slice(row0 + r, row0 + r + step)
        code, low = col_code[rows, :], col_low[rows, :]
        side = None
        for c, (lane_code, lane_low, _, _, both) in enumerate(lanes):
            here = score[r : r + step, c * LANES : (c + 1) * LANES]
            here = jnp.where(low == lane_low, here, -1.0)
            less = code < lane_code
            top = jnp.max(jnp.where(less, here, -1.0).reshape(step // 8, 8, LANES), axis=0)
            tops[c] = top if tops[c] is None else jnp.maximum(tops[c], top)
            if both:
                late = jnp.where(less, -1.0, here)
                side = late if side is None else jnp.maximum(side, late)
        if side is not None:
            col_best[rows, :] = jnp.maximum(col_best[rows, :], side)
    for top, (_, _, read, write, _) in zip(tops, lanes):
        write(jnp.maximum(read(), top))


def column_maxima(col_best):
    lines = col_best.shape[0] // LANES
    return jnp.concatenate(
        [
            jnp.max(col_best[t * LANES : (t + 1) * LANES, :].T, axis=0, keepdims=True)
            for t in range(lines)
        ],
        axis=0,
    )


def own_kernel(own_ref, out_ref, order, lane_code, lane_low, col_code, col_low, col_best, best, *scores):
    senders = own_ref.shape[0]
    count = senders * CAP
    size, most = scores[0].shape
    code = code_lines(own_ref, order)
    low = low_of(code)
    for t in range(count // LANES):
        lane_code[:, t * LANES : (t + 1) * LANES] = code[t : t + 1]
        lane_low[:, t * LANES : (t + 1) * LANES] = low[t : t + 1]
    code_columns(own_ref, col_code, col_low)
    col_best[...] = jnp.full(col_best.shape, -1.0, jnp.float32)
    best[...] = jnp.full(best.shape, -1.0, jnp.float32)

    def reduce(at, r0, c0, wide):
        lanes = []
        for c in range(c0, c0 + wide, LANES):
            span = slice(c, c + LANES)

            def read(span=span):
                return best[:, span]

            def write(x, span=span):
                best[:, span] = x

            lanes.append((lane_code[:, span], lane_low[:, span], read, write, c >= r0 + size))
        reduce_tile(scores[at], wide, r0, col_code, col_low, col_best, lanes)

    tiles = [
        (r0, c0, min(most, count - c0)) for r0 in range(0, count, size) for c0 in range(r0, count, most)
    ]
    for n, (r0, c0, wide) in enumerate(tiles):
        scores[n % 2][:, :wide] = lax.dot_general(
            rows_of(own_ref, r0 // CAP, size // CAP),
            rows_of(own_ref, c0 // CAP, wide // CAP),
            NT,
            preferred_element_type=jnp.float32,
        )
        if n:
            reduce((n - 1) % 2, *tiles[n - 1])
    reduce((len(tiles) - 1) % 2, *tiles[-1])
    top = jnp.max(best[...], axis=0, keepdims=True)
    top = jnp.concatenate([top[:, t : t + LANES] for t in range(0, count, LANES)], axis=0)
    out_ref[...] = jnp.maximum(top, column_maxima(col_best))


def cross_kernel(
    own_ref, other_ref, prev_ref, out_ref, order, lane_code, lane_low, col_code, col_low, col_best, best, *scores
):
    senders = own_ref.shape[0]
    count = senders * CAP
    size, most = scores[0].shape
    blocks = count // size
    each = size // LANES
    core = lax.axis_index("blk")
    code = code_lines(other_ref, order)
    low = low_of(code)
    for t in range(count // LANES):
        span = slice(t % each * LANES, (t % each + 1) * LANES)
        lane_code[t // each : t // each + 1, span] = code[t : t + 1]
        lane_low[t // each : t // each + 1, span] = low[t : t + 1]
    code_columns(own_ref, col_code, col_low)
    col_best[...] = jnp.full(col_best.shape, -1.0, jnp.float32)
    best[...] = jnp.full(best.shape, -1.0, jnp.float32)

    def others(n):
        return [lax.rem(n + core + k, blocks) for k in range(blocks // 2)]

    def reduce(n):
        lanes = []
        for j in others(n):
            code_here, low_here = lane_code[pl.ds(j, 1), :], lane_low[pl.ds(j, 1), :]
            for c in range(0, size, LANES):
                span = slice(c, c + LANES)

                def read(j=j, span=span):
                    return best[j, :, span]

                def write(x, j=j, span=span):
                    best[j, :, span] = x

                lanes.append((code_here[:, span], low_here[:, span], read, write, True))
        reduce_tile(scores[n % 2], most, n * size, col_code, col_low, col_best, lanes)

    for n in range(blocks):
        scores[n % 2][...] = lax.dot_general(
            rows_of(own_ref, n * size // CAP, size // CAP),
            jnp.concatenate(
                [rows_of(other_ref, j * (size // CAP), size // CAP) for j in others(n)], axis=0
            ),
            NT,
            preferred_element_type=jnp.float32,
        )
        if n:
            reduce(n - 1)
    reduce(blocks - 1)

    per = LANES // CAP
    lines = senders // per
    mine = jnp.maximum(prev_ref[...], column_maxima(col_best))
    theirs = jnp.concatenate(
        [
            jnp.max(best[t // each, :, t % each * LANES : (t % each + 1) * LANES], axis=0, keepdims=True)
            for t in range(lines)
        ],
        axis=0,
    )
    lane = lax.broadcasted_iota(jnp.int32, (lines, LANES), 1)
    for k in range(per):
        first = pltpu.roll(mine, (LANES - k * CAP) % LANES, 1) if k else mine
        second = pltpu.roll(theirs, (LANES + CAP - k * CAP) % LANES, 1) if k != 1 else theirs
        order[pl.ds(k, lines, stride=per), :] = jnp.where(lane < CAP, first, second)
    out_ref[...] = order[...]


def gram_call(kernel, out_shape, operands, blocked, senders, depth, pairs):
    count = senders * CAP
    size = min(512, count)
    most = min(1024, count)
    here = pl.BlockSpec(memory_space=pltpu.VMEM)
    lanes = (count // size, size) if blocked else (1, count)
    tops = (count // size, 8, size) if blocked else (8, count)
    return pl.pallas_call(
        kernel,
        in_specs=[here] * len(operands),
        out_specs=here,
        out_shape=jax.ShapeDtypeStruct(out_shape, jnp.float32),
        scratch_shapes=[
            pltpu.VMEM((senders, LANES), jnp.float32),
            pltpu.VMEM(lanes, jnp.float32),
            pltpu.VMEM(lanes, jnp.float32),
            pltpu.VMEM((count, LANES), jnp.float32),
            pltpu.VMEM((count, LANES), jnp.float32),
            pltpu.VMEM((count, LANES), jnp.float32),
            pltpu.VMEM(tops, jnp.float32),
            pltpu.VMEM((size, most), jnp.float32),
            pltpu.VMEM((size, most), jnp.float32),
        ],
        compiler_params=pltpu.CompilerParams(vmem_limit_bytes=24 << 20),
        cost_estimate=pl.CostEstimate(
            flops=2 * pairs * (depth // CAP) * LANES,
            bytes_accessed=4 * count * (depth // CAP) * LANES,
            transcendentals=0,
        ),
    )(*operands)


def unpack_kernel(back_ref, swap_ref, slot_ref, out_ref):
    groups = back_ref.shape[0]
    rows = slot_ref.shape[1]
    slot = slot_ref[...]
    group = lax.shift_right_logical(slot, 5)
    rank = slot & (CAP - 1)
    member = lax.broadcasted_iota(jnp.int32, (groups, rows), 0) == group
    member = jnp.where(member, 1.0, 0.0).astype(jnp.bfloat16)
    rest = jnp.maximum(back_ref[...], pltpu.roll(swap_ref[...], LANES - CAP, 1))
    found = jnp.zeros((LANES, rows), jnp.float32)
    for _ in range(3):
        piece = rest.astype(jnp.bfloat16)
        rest = rest - piece.astype(jnp.float32)
        found += lax.dot_general(
            piece, member, (((0,), (0,)), ((), ())), preferred_element_type=jnp.float32
        )
    chosen = lax.broadcasted_iota(jnp.int32, (CAP, rows), 0) == rank
    best = jnp.sum(jnp.where(chosen, found[:CAP], 0.0), axis=0, keepdims=True)
    out_ref[...] = jnp.concatenate(
        [best[:, b * LANES : (b + 1) * LANES] for b in range(rows // LANES)], axis=0
    )


def unpack(back, swap, slot):
    rows = slot.shape[1]
    return pl.pallas_call(
        unpack_kernel,
        out_shape=jax.ShapeDtypeStruct((rows // LANES, LANES), jnp.float32),
        compiler_params=pltpu.CompilerParams(vmem_limit_bytes=16 << 20),
    )(back, swap, slot)


def local(embeddings, labels, row_ids):
    groups = lax.axis_size("grp")
    rows = embeddings.shape[0]
    send, slot = pack(embeddings, labels, row_ids, groups)
    own = lax.all_to_all(send, "grp", split_axis=0, concat_axis=0, tiled=True)
    swap = [(0, 1), (1, 0)]
    other = lax.ppermute(own, "blk", swap)
    depth = own.shape[1]
    count = groups * CAP
    found = gram_call(
        own_kernel, (count // LANES, LANES), [own], False, groups, depth, count * count * 5 // 8
    )
    found = gram_call(
        cross_kernel, (groups, LANES), [own, other, found], True, groups, depth, count * count // 2
    )
    back = lax.all_to_all(found, "grp", split_axis=0, concat_axis=0, tiled=True)
    return unpack(back, lax.ppermute(back, "blk", swap), slot).reshape(rows)


def solution(mesh):
    in_specs = (P(("grp", "blk"), None), P(("grp", "blk")), P(("grp", "blk")))
    out_specs = P(("grp", "blk"))
    return jax.shard_map(local, mesh=mesh, in_specs=in_specs, out_specs=out_specs, check_vma=False)
```

```python
import functools

import jax
import jax.numpy as jnp
from jax import lax
from jax.experimental import pallas as pl
from jax.experimental.pallas import tpu as pltpu
from jax.sharding import PartitionSpec as P

CAP = 32
CL_GRP = 16
LANES = 128
PACK_ENDS = (4, 8, 12, 14, 16)
NT = (((1,), (1,)), ((), ()))


def pack_kernel(
    labels_ref, ids_ref, emb_ref, out_ref, slot_ref, lab, num, raw, unit, stage, slots, first, second, in_sems, out_sems, sems
):
    rows, width = unit.shape
    groups = out_ref.shape[0]
    lines = rows // LANES
    parts, blocks = in_sems.shape[0], out_sems.shape[0]
    part = rows // parts
    ends = [groups * n // 16 for n in PACK_ENDS]
    spans = list(zip([0] + ends[:-1], ends))
    fetch_labels = pltpu.make_async_copy(labels_ref, lab, sems.at[0])
    fetch_ids = pltpu.make_async_copy(ids_ref, num, sems.at[1])
    keep_slots = pltpu.make_async_copy(slots, slot_ref, sems.at[2])
    tail = width // LANES * CAP

    def load(p):
        span = pl.ds(p * part, part)
        return pltpu.make_async_copy(emb_ref.at[span], raw.at[span], in_sems.at[p])

    def store(n):
        span = pl.ds(spans[n][0], spans[n][1] - spans[n][0])
        return pltpu.make_async_copy(stage.at[span], out_ref.at[span], out_sems.at[n])

    fetch_labels.start()
    fetch_ids.start()
    for p in range(parts):
        load(p).start()

    fetch_labels.wait()
    labels = lab[...]
    place = (
        lax.broadcasted_iota(jnp.int32, (lines, LANES), 0) * LANES
        + lax.broadcasted_iota(jnp.int32, (lines, LANES), 1)
    )
    key = (labels * rows + place).astype(jnp.float32)
    target = lax.shift_right_logical(labels, 4)
    low = (target * (CL_GRP * rows)).astype(jnp.float32)
    tall = jnp.concatenate([key, jnp.zeros((LANES - lines, LANES), jnp.float32)], axis=0).T

    def flat(x):
        return jnp.concatenate([x[b : b + 1] for b in range(lines)], axis=1)

    key_row, low_row = flat(key), flat(low)
    count = jnp.zeros((LANES, rows), jnp.float32)
    for b in range(lines):
        col = tall[:, b : b + 1]
        count += jnp.where((col >= low_row) & (col < key_row), 1.0, 0.0)
    rank = jnp.sum(count, axis=0, keepdims=True).astype(jnp.int32)
    group = flat(target)
    slot = group * CAP + rank
    slots[...] = slot
    keep_slots.start()

    fetch_ids.wait()
    ids = num[...]
    pieces = [
        ids & 255,
        lax.shift_right_logical(ids, 8) & 255,
        (labels & (CL_GRP - 1)) * 2 + lax.shift_right_logical(ids, 16) + 1,
    ]
    ranked = lax.broadcasted_iota(jnp.int32, (CAP, rows), 0) == rank
    tags = [jnp.where(ranked, flat(x).astype(jnp.float32), 0.0) for x in pieces]
    tags.append(jnp.zeros((LANES - CAP * len(pieces), rows), jnp.float32))
    tags = jnp.concatenate(tags, axis=0).astype(jnp.bfloat16)
    member = lax.broadcasted_iota(jnp.int32, (LANES, rows), 0) == group
    member = jnp.where(member, 1.0, 0.0).astype(jnp.bfloat16)
    tags = lax.dot_general(member, tags, NT, preferred_element_type=jnp.float32)[:groups]
    stage[:, tail : tail + 8, :] = jnp.broadcast_to(
        tags.reshape(groups, 1, LANES), (groups, 8, LANES)
    ).astype(jnp.bfloat16)

    for p in range(parts):
        load(p).wait()
        wide = raw[p * part : (p + 1) * part].astype(jnp.float32)
        scale = lax.rsqrt(jnp.sum(wide * wide, axis=1, keepdims=True) + 1e-06)
        unit[p * part : (p + 1) * part] = (wide * scale).astype(jnp.bfloat16)

    sums = (first, second)

    def finish(n):
        at, end = spans[n]
        packed = sums[n % 2][: (end - at) * CAP].astype(jnp.bfloat16)
        for j in range(width // LANES):
            stage[at:end, j * CAP : (j + 1) * CAP, :] = packed[
                :, j * LANES : (j + 1) * LANES
            ].reshape(end - at, CAP, LANES)
        store(n).start()

    for n, (at, end) in enumerate(spans):
        size = (end - at) * CAP
        wanted = lax.broadcasted_iota(jnp.int32, (size, rows), 0) + at * CAP
        pick = jnp.where(slot == wanted, 1.0, 0.0).astype(jnp.bfloat16)
        sums[n % 2][:size] = jnp.dot(pick, unit[...], preferred_element_type=jnp.float32)
        if n:
            finish(n - 1)
    finish(blocks - 1)
    for n in range(blocks):
        store(n).wait()
    keep_slots.wait()


def pack(embeddings, labels, row_ids, groups):
    rows, width = embeddings.shape
    lines = rows // LANES
    depth = width // LANES * CAP + 8
    parts, blocks = 4, len(PACK_ENDS)
    there = pl.BlockSpec(memory_space=pl.ANY)
    return pl.pallas_call(
        pack_kernel,
        in_specs=[there] * 3,
        out_specs=[there] * 2,
        out_shape=[
            jax.ShapeDtypeStruct((groups, depth, LANES), jnp.bfloat16),
            jax.ShapeDtypeStruct((1, rows), jnp.int32),
        ],
        scratch_shapes=[
            pltpu.VMEM((lines, LANES), jnp.int32),
            pltpu.VMEM((lines, LANES), jnp.int32),
            pltpu.VMEM((rows, width), jnp.bfloat16),
            pltpu.VMEM((rows, width), jnp.bfloat16),
            pltpu.VMEM((groups, depth, LANES), jnp.bfloat16),
            pltpu.VMEM((1, rows), jnp.int32),
            pltpu.VMEM((groups // 2 * CAP, width), jnp.float32),
            pltpu.VMEM((groups // 2 * CAP, width), jnp.float32),
            pltpu.SemaphoreType.DMA((parts,)),
            pltpu.SemaphoreType.DMA((blocks,)),
            pltpu.SemaphoreType.DMA((3,)),
        ],
        compiler_params=pltpu.CompilerParams(vmem_limit_bytes=62 << 20),
        cost_estimate=pl.CostEstimate(
            flops=2 * groups * CAP * rows * width, bytes_accessed=6 * rows * width, transcendentals=rows
        ),
    )(labels.reshape(lines, LANES), row_ids.reshape(lines, LANES), embeddings)


def codes(block):
    tags = block.astype(jnp.float32)[:, 0, :]
    second, third = pltpu.roll(tags, LANES - CAP, 1), pltpu.roll(tags, LANES - 2 * CAP, 1)
    return (third - 1.0) * 65536.0 + second * 256.0 + tags


def low_of(code):
    return jnp.floor(code * (1.0 / 131072.0)) * 131072.0


def code_lines(ref, order):
    senders, depth, _ = ref.shape
    tail = depth // CAP * CAP
    per = LANES // CAP
    lines = senders // per
    lane = lax.broadcasted_iota(jnp.int32, (lines, LANES), 1)
    order[...] = codes(ref[:, tail : tail + 8, :])
    code = order[pl.ds(0, lines, stride=per), :]
    for k in range(1, per):
        turned = pltpu.roll(order[pl.ds(k, lines, stride=per), :], k * CAP, 1)
        code = jnp.where(lane >= k * CAP, turned, code)
    return code


def code_columns(ref, col_code, col_low):
    senders, depth, _ = ref.shape
    tail = depth // CAP * CAP
    tall = codes(ref[:, tail : tail + 8, :])
    tall = jnp.concatenate([tall, jnp.zeros((LANES - senders, LANES), jnp.float32)], axis=0).T
    for s in range(senders):
        col = jnp.broadcast_to(tall[:CAP, s : s + 1], (CAP, LANES))
        col_code[s * CAP : (s + 1) * CAP, :] = col
        col_low[s * CAP : (s + 1) * CAP, :] = low_of(col)


def rows_of(ref, sender, count):
    chunks = ref.shape[1] // CAP
    return jnp.concatenate(
        [
            ref[pl.ds(sender, count), j * CAP : (j + 1) * CAP, :].reshape(count * CAP, LANES)
            for j in range(chunks)
        ],
        axis=1,
    )


def reduce_tile(score, wide, row0, col_code, col_low, col_best, lanes):
    size = score.shape[0]
    step = 64
    tops = [None] * (wide // LANES)
    for r in range(0, size, step):
        rows = slice(row0 + r, row0 + r + step)
        code, low = col_code[rows, :], col_low[rows, :]
        side = None
        for c, (lane_code, lane_low, _, _, both) in enumerate(lanes):
            here = score[r : r + step, c * LANES : (c + 1) * LANES]
            here = jnp.where(low == lane_low, here, -1.0)
            less = code < lane_code
            top = jnp.max(jnp.where(less, here, -1.0).reshape(step // 8, 8, LANES), axis=0)
            tops[c] = top if tops[c] is None else jnp.maximum(tops[c], top)
            if both:
                late = jnp.where(less, -1.0, here)
                side = late if side is None else jnp.maximum(side, late)
        if side is not None:
            col_best[rows, :] = jnp.maximum(col_best[rows, :], side)
    for top, (_, _, read, write, _) in zip(tops, lanes):
        write(jnp.maximum(read(), top))


def column_maxima(col_best, row0, size):
    return [
        jnp.max(col_best[t : t + LANES, :].T, axis=0, keepdims=True)
        for t in range(row0, row0 + size, LANES)
    ]


def own_kernel(own_ref, out_ref, col_code, col_low, order, lane_code, lane_low, col_best, best, *scores):
    senders = own_ref.shape[0]
    count = senders * CAP
    size, most = scores[0].shape

    def prepare():
        code = code_lines(own_ref, order)
        low = low_of(code)
        for t in range(count // LANES):
            lane_code[:, t * LANES : (t + 1) * LANES] = code[t : t + 1]
            lane_low[:, t * LANES : (t + 1) * LANES] = low[t : t + 1]
        code_columns(own_ref, col_code, col_low)
        col_best[...] = jnp.full(col_best.shape, -1.0, jnp.float32)
        best[...] = jnp.full(best.shape, -1.0, jnp.float32)

    def reduce(at, r0, c0, wide):
        lanes = []
        for c in range(c0, c0 + wide, LANES):
            span = slice(c, c + LANES)

            def read(span=span):
                return best[:, span]

            def write(x, span=span):
                best[:, span] = x

            lanes.append((lane_code[:, span], lane_low[:, span], read, write, c >= r0 + size))
        reduce_tile(scores[at], wide, r0, col_code, col_low, col_best, lanes)

    tiles = [
        (r0, c0, min(most, count - c0)) for r0 in range(0, count, size) for c0 in range(r0, count, most)
    ]
    tops = []
    for n in range(len(tiles) + 1):
        if n < len(tiles):
            r0, c0, wide = tiles[n]
            scores[n % 2][:, :wide] = lax.dot_general(
                rows_of(own_ref, r0 // CAP, size // CAP),
                rows_of(own_ref, c0 // CAP, wide // CAP),
                NT,
                preferred_element_type=jnp.float32,
            )
        if n == 0:
            prepare()
            continue
        r0, c0, wide = tiles[n - 1]
        reduce((n - 1) % 2, r0, c0, wide)
        if c0 + wide == count:
            tops += column_maxima(col_best, r0, size)
    top = jnp.max(best[...], axis=0, keepdims=True)
    top = jnp.concatenate([top[:, t : t + LANES] for t in range(0, count, LANES)], axis=0)
    out_ref[...] = jnp.maximum(top, jnp.concatenate(tops, axis=0))


def cross_kernel(
    own_ref, other_ref, prev_ref, col_code, col_low, out_ref, order, lane_code, lane_low, col_best, best, *scores
):
    senders = own_ref.shape[0]
    count = senders * CAP
    size, most = scores[0].shape
    blocks = count // size
    each = size // LANES
    core = lax.axis_index("blk")

    def prepare():
        code = code_lines(other_ref, order)
        low = low_of(code)
        for t in range(count // LANES):
            span = slice(t % each * LANES, (t % each + 1) * LANES)
            lane_code[t // each : t // each + 1, span] = code[t : t + 1]
            lane_low[t // each : t // each + 1, span] = low[t : t + 1]
        col_best[...] = jnp.full(col_best.shape, -1.0, jnp.float32)
        best[...] = jnp.full(best.shape, -1.0, jnp.float32)

    def reduce(at, n, others):
        lanes = []
        for j in others:
            code_here, low_here = lane_code[pl.ds(j, 1), :], lane_low[pl.ds(j, 1), :]
            for c in range(0, size, LANES):
                span = slice(c, c + LANES)

                def read(j=j, span=span):
                    return best[j, :, span]

                def write(x, j=j, span=span):
                    best[j, :, span] = x

                lanes.append((code_here[:, span], low_here[:, span], read, write, True))
        reduce_tile(scores[at], len(others) * size, n * size, col_code, col_low, col_best, lanes)

    tiles = [(n, [lax.rem(n + core + k, blocks) for k in range(blocks // 2)]) for n in range(blocks)]
    tiles = tiles[:-1] + [(blocks - 1, [j]) for j in tiles[-1][1]]
    tops = []
    for t in range(len(tiles) + 1):
        if t < len(tiles):
            n, others = tiles[t]
            scores[t % 2][:, : len(others) * size] = lax.dot_general(
                rows_of(own_ref, n * size // CAP, size // CAP),
                jnp.concatenate(
                    [rows_of(other_ref, j * (size // CAP), size // CAP) for j in others], axis=0
                ),
                NT,
                preferred_element_type=jnp.float32,
            )
        if t == 0:
            prepare()
            continue
        n, others = tiles[t - 1]
        reduce((t - 1) % 2, n, others)
        if t == len(tiles) or tiles[t][0] != n:
            tops += column_maxima(col_best, n * size, size)

    per = LANES // CAP
    lines = senders // per
    mine = jnp.maximum(prev_ref[...], jnp.concatenate(tops, axis=0))
    theirs = jnp.concatenate(
        [
            jnp.max(best[t // each, :, t % each * LANES : (t % each + 1) * LANES], axis=0, keepdims=True)
            for t in range(lines)
        ],
        axis=0,
    )
    lane = lax.broadcasted_iota(jnp.int32, (lines, LANES), 1)
    for k in range(per):
        first = pltpu.roll(mine, LANES - k * CAP, 1) if k else mine
        second = pltpu.roll(theirs, (LANES + CAP - k * CAP) % LANES, 1) if k != 1 else theirs
        order[pl.ds(k, lines, stride=per), :] = jnp.where(lane < CAP, first, second)
    out_ref[...] = order[...]


def gram_call(kernel, out_shapes, operands, blocked, senders, depth, pairs):
    count = senders * CAP
    size = min(512, count)
    most = min(1024, count)
    here = pl.BlockSpec(memory_space=pltpu.VMEM)
    lanes = (count // size, size) if blocked else (1, count)
    tops = (count // size, 8, size) if blocked else (8, count)
    return pl.pallas_call(
        kernel,
        in_specs=[here] * len(operands),
        out_specs=[here] * len(out_shapes),
        out_shape=[jax.ShapeDtypeStruct(shape, jnp.float32) for shape in out_shapes],
        scratch_shapes=[
            pltpu.VMEM((senders, LANES), jnp.float32),
            pltpu.VMEM(lanes, jnp.float32),
            pltpu.VMEM(lanes, jnp.float32),
            pltpu.VMEM((count, LANES), jnp.float32),
            pltpu.VMEM(tops, jnp.float32),
            pltpu.VMEM((size, most), jnp.float32),
            pltpu.VMEM((size, most), jnp.float32),
        ],
        compiler_params=pltpu.CompilerParams(vmem_limit_bytes=24 << 20),
        cost_estimate=pl.CostEstimate(
            flops=2 * pairs * (depth // CAP) * LANES,
            bytes_accessed=4 * count * (depth // CAP) * LANES,
            transcendentals=0,
        ),
    )(*operands)


def unpack_kernel(back_ref, swap_ref, slot_ref, out_ref):
    groups = back_ref.shape[0]
    rows = slot_ref.shape[1]
    slot = slot_ref[...]
    group = lax.shift_right_logical(slot, 5)
    rank = slot & (CAP - 1)
    member = lax.broadcasted_iota(jnp.int32, (groups, rows), 0) == group
    member = jnp.where(member, 1.0, 0.0).astype(jnp.bfloat16)
    rest = jnp.maximum(back_ref[...], pltpu.roll(swap_ref[...], LANES - CAP, 1))
    found = jnp.zeros((LANES, rows), jnp.float32)
    for _ in range(3):
        piece = rest.astype(jnp.bfloat16)
        rest = rest - piece.astype(jnp.float32)
        found += lax.dot_general(
            piece, member, (((0,), (0,)), ((), ())), preferred_element_type=jnp.float32
        )
    chosen = lax.broadcasted_iota(jnp.int32, (CAP, rows), 0) == rank
    best = jnp.sum(jnp.where(chosen, found[:CAP], 0.0), axis=0, keepdims=True)
    out_ref[...] = jnp.concatenate(
        [best[:, b * LANES : (b + 1) * LANES] for b in range(rows // LANES)], axis=0
    )


def unpack(back, swap, slot):
    rows = slot.shape[1]
    return pl.pallas_call(
        unpack_kernel,
        out_shape=jax.ShapeDtypeStruct((rows // LANES, LANES), jnp.float32),
        compiler_params=pltpu.CompilerParams(vmem_limit_bytes=16 << 20),
    )(back, swap, slot)


def local(embeddings, labels, row_ids):
    groups = lax.axis_size("grp")
    rows = embeddings.shape[0]
    send, slot = pack(embeddings, labels, row_ids, groups)
    own = lax.all_to_all(send, "grp", split_axis=0, concat_axis=0, tiled=True)
    swap = [(0, 1), (1, 0)]
    other = lax.ppermute(own, "blk", swap)
    depth = own.shape[1]
    count = groups * CAP
    found, col_code, col_low = gram_call(
        own_kernel,
        [(count // LANES, LANES), (count, LANES), (count, LANES)],
        [own],
        False,
        groups,
        depth,
        count * count * 5 // 8,
    )
    [found] = gram_call(
        cross_kernel,
        [(groups, LANES)],
        [own, other, found, col_code, col_low],
        True,
        groups,
        depth,
        count * count // 2,
    )
    back = lax.all_to_all(found, "grp", split_axis=0, concat_axis=0, tiled=True)
    return unpack(back, lax.ppermute(back, "blk", swap), slot).reshape(rows)


def solution(mesh):
    in_specs = (P(("grp", "blk"), None), P(("grp", "blk")), P(("grp", "blk")))
    out_specs = P(("grp", "blk"))
    return jax.shard_map(local, mesh=mesh, in_specs=in_specs, out_specs=out_specs, check_vma=False)
```

```python
import functools

import jax
import jax.numpy as jnp
from jax import lax
from jax.experimental import pallas as pl
from jax.experimental.pallas import tpu as pltpu
from jax.sharding import PartitionSpec as P

CAP = 32
CL_GRP = 16
LANES = 128
PACK_ENDS = (8, 13, 15, 16)
NT = (((1,), (1,)), ((), ()))


def pack_kernel(
    labels_ref, ids_ref, emb_ref, out_ref, slot_ref, lab, num, raw, unit, stage, slots, first, second, in_sems, out_sems, sems
):
    rows, width = unit.shape
    groups = out_ref.shape[0]
    lines = rows // LANES
    parts, blocks = in_sems.shape[0], out_sems.shape[0]
    part = rows // parts
    ends = [groups * n // 16 for n in PACK_ENDS]
    spans = list(zip([0] + ends[:-1], ends))
    fetch_labels = pltpu.make_async_copy(labels_ref, lab, sems.at[0])
    fetch_ids = pltpu.make_async_copy(ids_ref, num, sems.at[1])
    keep_slots = pltpu.make_async_copy(slots, slot_ref, sems.at[2])
    tail = width // LANES * CAP

    def load(p):
        span = pl.ds(p * part, part)
        return pltpu.make_async_copy(emb_ref.at[span], raw.at[span], in_sems.at[p])

    def store(n):
        span = pl.ds(spans[n][0], spans[n][1] - spans[n][0])
        return pltpu.make_async_copy(stage.at[span], out_ref.at[span], out_sems.at[n])

    fetch_labels.start()
    fetch_ids.start()
    for p in range(parts):
        load(p).start()

    fetch_labels.wait()
    labels = lab[...]
    place = (
        lax.broadcasted_iota(jnp.int32, (lines, LANES), 0) * LANES
        + lax.broadcasted_iota(jnp.int32, (lines, LANES), 1)
    )
    key = (labels * rows + place).astype(jnp.float32)
    target = lax.shift_right_logical(labels, 4)
    low = (target * (CL_GRP * rows)).astype(jnp.float32)
    tall = jnp.concatenate([key, jnp.zeros((LANES - lines, LANES), jnp.float32)], axis=0).T

    def flat(x):
        return jnp.concatenate([x[b : b + 1] for b in range(lines)], axis=1)

    key_row, low_row = flat(key), flat(low)
    count = jnp.zeros((LANES, rows), jnp.float32)
    for b in range(lines):
        col = tall[:, b : b + 1]
        count += jnp.where((col >= low_row) & (col < key_row), 1.0, 0.0)
    rank = jnp.sum(count, axis=0, keepdims=True).astype(jnp.int32)
    group = flat(target)
    slot = group * CAP + rank
    slots[...] = slot
    keep_slots.start()

    fetch_ids.wait()
    ids = num[...]
    pieces = [
        ids & 255,
        lax.shift_right_logical(ids, 8) & 255,
        (labels & (CL_GRP - 1)) * 2 + lax.shift_right_logical(ids, 16) + 1,
    ]
    ranked = lax.broadcasted_iota(jnp.int32, (CAP, rows), 0) == rank
    tags = [jnp.where(ranked, flat(x).astype(jnp.float32), 0.0) for x in pieces]
    tags.append(jnp.zeros((LANES - CAP * len(pieces), rows), jnp.float32))
    tags = jnp.concatenate(tags, axis=0).astype(jnp.bfloat16)
    member = lax.broadcasted_iota(jnp.int32, (LANES, rows), 0) == group
    member = jnp.where(member, 1.0, 0.0).astype(jnp.bfloat16)
    tags = lax.dot_general(member, tags, NT, preferred_element_type=jnp.float32)[:groups]
    stage[:, tail : tail + 8, :] = jnp.broadcast_to(
        tags.reshape(groups, 1, LANES), (groups, 8, LANES)
    ).astype(jnp.bfloat16)

    for p in range(parts):
        load(p).wait()
        wide = raw[p * part : (p + 1) * part].astype(jnp.float32)
        scale = lax.rsqrt(jnp.sum(wide * wide, axis=1, keepdims=True) + 1e-06)
        unit[p * part : (p + 1) * part] = (wide * scale).astype(jnp.bfloat16)

    sums = (first, second)

    def finish(n):
        at, end = spans[n]
        packed = sums[n % 2][: (end - at) * CAP].astype(jnp.bfloat16)
        for j in range(width // LANES):
            stage[at:end, j * CAP : (j + 1) * CAP, :] = packed[
                :, j * LANES : (j + 1) * LANES
            ].reshape(end - at, CAP, LANES)
        store(n).start()

    for n, (at, end) in enumerate(spans):
        size = (end - at) * CAP
        wanted = lax.broadcasted_iota(jnp.int32, (size, rows), 0) + at * CAP
        pick = jnp.where(slot == wanted, 1.0, 0.0).astype(jnp.bfloat16)
        sums[n % 2][:size] = jnp.dot(pick, unit[...], preferred_element_type=jnp.float32)
        if n:
            finish(n - 1)
    finish(blocks - 1)
    for n in range(blocks):
        store(n).wait()
    keep_slots.wait()


def pack(embeddings, labels, row_ids, groups):
    rows, width = embeddings.shape
    lines = rows // LANES
    depth = width // LANES * CAP + 8
    parts, blocks = 1, len(PACK_ENDS)
    there = pl.BlockSpec(memory_space=pl.ANY)
    return pl.pallas_call(
        pack_kernel,
        in_specs=[there] * 3,
        out_specs=[there] * 2,
        out_shape=[
            jax.ShapeDtypeStruct((groups, depth, LANES), jnp.bfloat16),
            jax.ShapeDtypeStruct((1, rows), jnp.int32),
        ],
        scratch_shapes=[
            pltpu.VMEM((lines, LANES), jnp.int32),
            pltpu.VMEM((lines, LANES), jnp.int32),
            pltpu.VMEM((rows, width), jnp.bfloat16),
            pltpu.VMEM((rows, width), jnp.bfloat16),
            pltpu.VMEM((groups, depth, LANES), jnp.bfloat16),
            pltpu.VMEM((1, rows), jnp.int32),
            pltpu.VMEM((groups * 3 // 4 * CAP, width), jnp.float32),
            pltpu.VMEM((groups * 3 // 4 * CAP, width), jnp.float32),
            pltpu.SemaphoreType.DMA((parts,)),
            pltpu.SemaphoreType.DMA((blocks,)),
            pltpu.SemaphoreType.DMA((3,)),
        ],
        compiler_params=pltpu.CompilerParams(vmem_limit_bytes=62 << 20),
        cost_estimate=pl.CostEstimate(
            flops=2 * groups * CAP * rows * width, bytes_accessed=6 * rows * width, transcendentals=rows
        ),
    )(labels.reshape(lines, LANES), row_ids.reshape(lines, LANES), embeddings)


def codes(block):
    tags = block.astype(jnp.float32)[:, 0, :]
    second, third = pltpu.roll(tags, LANES - CAP, 1), pltpu.roll(tags, LANES - 2 * CAP, 1)
    return (third - 1.0) * 65536.0 + second * 256.0 + tags


def low_of(code):
    return jnp.floor(code * (1.0 / 131072.0)) * 131072.0


def code_lines(ref, order):
    senders, depth, _ = ref.shape
    tail = depth // CAP * CAP
    per = LANES // CAP
    lines = senders // per
    lane = lax.broadcasted_iota(jnp.int32, (lines, LANES), 1)
    order[...] = codes(ref[:, tail : tail + 8, :])
    code = order[pl.ds(0, lines, stride=per), :]
    for k in range(1, per):
        turned = pltpu.roll(order[pl.ds(k, lines, stride=per), :], k * CAP, 1)
        code = jnp.where(lane >= k * CAP, turned, code)
    return code


def code_columns(ref, col_code, col_low):
    senders, depth, _ = ref.shape
    tail = depth // CAP * CAP
    tall = codes(ref[:, tail : tail + 8, :])
    tall = jnp.concatenate([tall, jnp.zeros((LANES - senders, LANES), jnp.float32)], axis=0).T
    for s in range(senders):
        col = jnp.broadcast_to(tall[:CAP, s : s + 1], (CAP, LANES))
        col_code[s * CAP : (s + 1) * CAP, :] = col
        col_low[s * CAP : (s + 1) * CAP, :] = low_of(col)


def rows_of(ref, sender, count):
    chunks = ref.shape[1] // CAP
    return jnp.concatenate(
        [
            ref[pl.ds(sender, count), j * CAP : (j + 1) * CAP, :].reshape(count * CAP, LANES)
            for j in range(chunks)
        ],
        axis=1,
    )


def reduce_tile(score, wide, row0, col_code, col_low, col_best, lanes):
    size = score.shape[0]
    step = 64
    tops = [None] * (wide // LANES)
    for r in range(0, size, step):
        rows = slice(row0 + r, row0 + r + step)
        code, low = col_code[rows, :], col_low[rows, :]
        side = None
        for c, (lane_code, lane_low, _, _, both) in enumerate(lanes):
            here = score[r : r + step, c * LANES : (c + 1) * LANES]
            here = jnp.where(low == lane_low, here, -1.0)
            less = code < lane_code
            top = jnp.max(jnp.where(less, here, -1.0).reshape(step // 8, 8, LANES), axis=0)
            tops[c] = top if tops[c] is None else jnp.maximum(tops[c], top)
            if both:
                late = jnp.where(less, -1.0, here)
                side = late if side is None else jnp.maximum(side, late)
        if side is not None:
            col_best[rows, :] = jnp.maximum(col_best[rows, :], side)
    for top, (_, _, read, write, _) in zip(tops, lanes):
        write(jnp.maximum(read(), top))


def column_maxima(col_best, row0, size):
    return [
        jnp.max(col_best[t : t + LANES, :].T, axis=0, keepdims=True)
        for t in range(row0, row0 + size, LANES)
    ]


def own_kernel(own_ref, out_ref, col_code, col_low, order, lane_code, lane_low, col_best, best, *scores):
    senders = own_ref.shape[0]
    count = senders * CAP
    size, most = scores[0].shape

    def prepare():
        code = code_lines(own_ref, order)
        low = low_of(code)
        for t in range(count // LANES):
            lane_code[:, t * LANES : (t + 1) * LANES] = code[t : t + 1]
            lane_low[:, t * LANES : (t + 1) * LANES] = low[t : t + 1]
        code_columns(own_ref, col_code, col_low)
        col_best[...] = jnp.full(col_best.shape, -1.0, jnp.float32)
        best[...] = jnp.full(best.shape, -1.0, jnp.float32)

    def reduce(at, r0, c0, wide):
        lanes = []
        for c in range(c0, c0 + wide, LANES):
            span = slice(c, c + LANES)

            def read(span=span):
                return best[:, span]

            def write(x, span=span):
                best[:, span] = x

            lanes.append((lane_code[:, span], lane_low[:, span], read, write, c >= r0 + size))
        reduce_tile(scores[at], wide, r0, col_code, col_low, col_best, lanes)

    tiles = [
        (r0, c0, min(most, count - c0)) for r0 in range(0, count, size) for c0 in range(r0, count, most)
    ]
    tops = []
    for n in range(len(tiles) + 1):
        if n < len(tiles):
            r0, c0, wide = tiles[n]
            scores[n % 2][:, :wide] = lax.dot_general(
                rows_of(own_ref, r0 // CAP, size // CAP),
                rows_of(own_ref, c0 // CAP, wide // CAP),
                NT,
                preferred_element_type=jnp.float32,
            )
        if n == 0:
            prepare()
            continue
        r0, c0, wide = tiles[n - 1]
        reduce((n - 1) % 2, r0, c0, wide)
        if c0 + wide == count:
            tops += column_maxima(col_best, r0, size)
    top = jnp.max(best[...], axis=0, keepdims=True)
    top = jnp.concatenate([top[:, t : t + LANES] for t in range(0, count, LANES)], axis=0)
    out_ref[...] = jnp.maximum(top, jnp.concatenate(tops, axis=0))


def cross_kernel(
    own_ref, other_ref, prev_ref, col_code, col_low, out_ref, order, lane_code, lane_low, col_best, best, *scores
):
    senders = own_ref.shape[0]
    count = senders * CAP
    size, most = scores[0].shape
    blocks = count // size
    each = size // LANES
    core = lax.axis_index("blk")

    def prepare():
        code = code_lines(other_ref, order)
        low = low_of(code)
        for t in range(count // LANES):
            span = slice(t % each * LANES, (t % each + 1) * LANES)
            lane_code[t // each : t // each + 1, span] = code[t : t + 1]
            lane_low[t // each : t // each + 1, span] = low[t : t + 1]
        col_best[...] = jnp.full(col_best.shape, -1.0, jnp.float32)
        best[...] = jnp.full(best.shape, -1.0, jnp.float32)

    def reduce(at, n, others):
        lanes = []
        for j in others:
            code_here, low_here = lane_code[pl.ds(j, 1), :], lane_low[pl.ds(j, 1), :]
            for c in range(0, size, LANES):
                span = slice(c, c + LANES)

                def read(j=j, span=span):
                    return best[j, :, span]

                def write(x, j=j, span=span):
                    best[j, :, span] = x

                lanes.append((code_here[:, span], low_here[:, span], read, write, True))
        reduce_tile(scores[at], len(others) * size, n * size, col_code, col_low, col_best, lanes)

    tiles = [(n, [lax.rem(n + core + k, blocks) for k in range(blocks // 2)]) for n in range(blocks)]
    tiles = tiles[:-1] + [(blocks - 1, [j]) for j in tiles[-1][1]]
    tops = []
    for t in range(len(tiles) + 1):
        if t < len(tiles):
            n, others = tiles[t]
            scores[t % 2][:, : len(others) * size] = lax.dot_general(
                rows_of(own_ref, n * size // CAP, size // CAP),
                jnp.concatenate(
                    [rows_of(other_ref, j * (size // CAP), size // CAP) for j in others], axis=0
                ),
                NT,
                preferred_element_type=jnp.float32,
            )
        if t == 0:
            prepare()
            continue
        n, others = tiles[t - 1]
        reduce((t - 1) % 2, n, others)
        if t == len(tiles) or tiles[t][0] != n:
            tops += column_maxima(col_best, n * size, size)

    per = LANES // CAP
    lines = senders // per
    mine = jnp.maximum(prev_ref[...], jnp.concatenate(tops, axis=0))
    theirs = jnp.concatenate(
        [
            jnp.max(best[t // each, :, t % each * LANES : (t % each + 1) * LANES], axis=0, keepdims=True)
            for t in range(lines)
        ],
        axis=0,
    )
    lane = lax.broadcasted_iota(jnp.int32, (lines, LANES), 1)
    for k in range(per):
        first = pltpu.roll(mine, LANES - k * CAP, 1) if k else mine
        second = pltpu.roll(theirs, (LANES + CAP - k * CAP) % LANES, 1) if k != 1 else theirs
        order[pl.ds(k, lines, stride=per), :] = jnp.where(lane < CAP, first, second)
    out_ref[...] = order[...]


def gram_call(kernel, out_shapes, operands, blocked, senders, depth, pairs):
    count = senders * CAP
    size = min(512, count)
    most = min(1024, count)
    here = pl.BlockSpec(memory_space=pltpu.VMEM)
    lanes = (count // size, size) if blocked else (1, count)
    tops = (count // size, 8, size) if blocked else (8, count)
    return pl.pallas_call(
        kernel,
        in_specs=[here] * len(operands),
        out_specs=[here] * len(out_shapes),
        out_shape=[jax.ShapeDtypeStruct(shape, jnp.float32) for shape in out_shapes],
        scratch_shapes=[
            pltpu.VMEM((senders, LANES), jnp.float32),
            pltpu.VMEM(lanes, jnp.float32),
            pltpu.VMEM(lanes, jnp.float32),
            pltpu.VMEM((count, LANES), jnp.float32),
            pltpu.VMEM(tops, jnp.float32),
            pltpu.VMEM((size, most), jnp.float32),
            pltpu.VMEM((size, most), jnp.float32),
        ],
        compiler_params=pltpu.CompilerParams(vmem_limit_bytes=24 << 20),
        cost_estimate=pl.CostEstimate(
            flops=2 * pairs * (depth // CAP) * LANES,
            bytes_accessed=4 * count * (depth // CAP) * LANES,
            transcendentals=0,
        ),
    )(*operands)


def unpack_kernel(back_ref, swap_ref, slot_ref, out_ref):
    groups = back_ref.shape[0]
    rows = slot_ref.shape[1]
    slot = slot_ref[...]
    group = lax.shift_right_logical(slot, 5)
    rank = slot & (CAP - 1)
    member = lax.broadcasted_iota(jnp.int32, (groups, rows), 0) == group
    member = jnp.where(member, 1.0, 0.0).astype(jnp.bfloat16)
    rest = jnp.maximum(back_ref[...], pltpu.roll(swap_ref[...], LANES - CAP, 1))
    found = jnp.zeros((LANES, rows), jnp.float32)
    for _ in range(3):
        piece = rest.astype(jnp.bfloat16)
        rest = rest - piece.astype(jnp.float32)
        found += lax.dot_general(
            piece, member, (((0,), (0,)), ((), ())), preferred_element_type=jnp.float32
        )
    chosen = lax.broadcasted_iota(jnp.int32, (CAP, rows), 0) == rank
    best = jnp.sum(jnp.where(chosen, found[:CAP], 0.0), axis=0, keepdims=True)
    out_ref[...] = jnp.concatenate(
        [best[:, b * LANES : (b + 1) * LANES] for b in range(rows // LANES)], axis=0
    )


def unpack(back, swap, slot):
    rows = slot.shape[1]
    return pl.pallas_call(
        unpack_kernel,
        out_shape=jax.ShapeDtypeStruct((rows // LANES, LANES), jnp.float32),
        compiler_params=pltpu.CompilerParams(vmem_limit_bytes=16 << 20),
    )(back, swap, slot)


def local(embeddings, labels, row_ids):
    groups = lax.axis_size("grp")
    rows = embeddings.shape[0]
    send, slot = pack(embeddings, labels, row_ids, groups)
    own = lax.all_to_all(send, "grp", split_axis=0, concat_axis=0, tiled=True)
    swap = [(0, 1), (1, 0)]
    other = lax.ppermute(own, "blk", swap)
    depth = own.shape[1]
    count = groups * CAP
    found, col_code, col_low = gram_call(
        own_kernel,
        [(count // LANES, LANES), (count, LANES), (count, LANES)],
        [own],
        False,
        groups,
        depth,
        count * count * 5 // 8,
    )
    [found] = gram_call(
        cross_kernel,
        [(groups, LANES)],
        [own, other, found, col_code, col_low],
        True,
        groups,
        depth,
        count * count // 2,
    )
    back = lax.all_to_all(found, "grp", split_axis=0, concat_axis=0, tiled=True)
    return unpack(back, lax.ppermute(back, "blk", swap), slot).reshape(rows)


def solution(mesh):
    in_specs = (P(("grp", "blk"), None), P(("grp", "blk")), P(("grp", "blk")))
    out_specs = P(("grp", "blk"))
    return jax.shard_map(local, mesh=mesh, in_specs=in_specs, out_specs=out_specs, check_vma=False)
```

```python
import functools

import jax
import jax.numpy as jnp
from jax import lax
from jax.experimental import pallas as pl
from jax.experimental.pallas import tpu as pltpu
from jax.sharding import PartitionSpec as P

CAP = 32
CL_GRP = 16
LANES = 128
PACK_ENDS = (8, 13, 15, 16)
NT = (((1,), (1,)), ((), ()))


def pack_kernel(
    labels_ref, ids_ref, emb_ref, out_ref, slot_ref, lab, num, raw, unit, stage, slots, first, second, in_sems, out_sems, sems
):
    rows, width = unit.shape
    groups = out_ref.shape[0]
    lines = rows // LANES
    parts, blocks = in_sems.shape[0], out_sems.shape[0]
    part = rows // parts
    ends = [groups * n // 16 for n in PACK_ENDS]
    spans = list(zip([0] + ends[:-1], ends))
    fetch_labels = pltpu.make_async_copy(labels_ref, lab, sems.at[0])
    fetch_ids = pltpu.make_async_copy(ids_ref, num, sems.at[1])
    keep_slots = pltpu.make_async_copy(slots, slot_ref, sems.at[2])
    tail = width // LANES * CAP

    def load(p):
        span = pl.ds(p * part, part)
        return pltpu.make_async_copy(emb_ref.at[span], raw.at[span], in_sems.at[p])

    def store(n):
        span = pl.ds(spans[n][0], spans[n][1] - spans[n][0])
        return pltpu.make_async_copy(stage.at[span], out_ref.at[span], out_sems.at[n])

    fetch_labels.start()
    fetch_ids.start()
    for p in range(parts):
        load(p).start()

    fetch_labels.wait()
    fetch_ids.wait()
    labels = lab[...]
    place = (
        lax.broadcasted_iota(jnp.int32, (lines, LANES), 0) * LANES
        + lax.broadcasted_iota(jnp.int32, (lines, LANES), 1)
    )
    key = (labels * rows + place).astype(jnp.float32)
    target = lax.shift_right_logical(labels, 4)
    low = (target * (CL_GRP * rows)).astype(jnp.float32)
    tall = jnp.concatenate([key, jnp.zeros((LANES - lines, LANES), jnp.float32)], axis=0).T

    def flat(x):
        return jnp.concatenate([x[b : b + 1] for b in range(lines)], axis=1)

    key_row, low_row = flat(key), flat(low)
    count = jnp.zeros((LANES, rows), jnp.float32)
    for b in range(lines):
        col = tall[:, b : b + 1]
        count += jnp.where((col >= low_row) & (col < key_row), 1.0, 0.0)
    rank = jnp.sum(count, axis=0, keepdims=True).astype(jnp.int32)
    group = flat(target)
    slot = group * CAP + rank
    slots[...] = slot

    ids = num[...]
    pieces = [
        ids & 255,
        lax.shift_right_logical(ids, 8) & 255,
        (labels & (CL_GRP - 1)) * 2 + lax.shift_right_logical(ids, 16) + 1,
    ]
    ranked = lax.broadcasted_iota(jnp.int32, (CAP, rows), 0) == rank
    tags = [jnp.where(ranked, flat(x).astype(jnp.float32), 0.0) for x in pieces]
    tags.append(jnp.zeros((LANES - CAP * len(pieces), rows), jnp.float32))
    tags = jnp.concatenate(tags, axis=0).astype(jnp.bfloat16)
    member = lax.broadcasted_iota(jnp.int32, (LANES, rows), 0) == group
    member = jnp.where(member, 1.0, 0.0).astype(jnp.bfloat16)
    tags = lax.dot_general(member, tags, NT, preferred_element_type=jnp.float32)[:groups]
    stage[:, tail : tail + 8, :] = jnp.broadcast_to(
        tags.reshape(groups, 1, LANES), (groups, 8, LANES)
    ).astype(jnp.bfloat16)

    for p in range(parts):
        load(p).wait()
        wide = raw[p * part : (p + 1) * part].astype(jnp.float32)
        scale = lax.rsqrt(jnp.sum(wide * wide, axis=1, keepdims=True) + 1e-06)
        unit[p * part : (p + 1) * part] = (wide * scale).astype(jnp.bfloat16)

    sums = (first, second)

    def finish(n):
        at, end = spans[n]
        packed = sums[n % 2][: (end - at) * CAP].astype(jnp.bfloat16)
        for j in range(width // LANES):
            stage[at:end, j * CAP : (j + 1) * CAP, :] = packed[
                :, j * LANES : (j + 1) * LANES
            ].reshape(end - at, CAP, LANES)
        store(n).start()
        if n == 0:
            keep_slots.start()

    for n, (at, end) in enumerate(spans):
        size = (end - at) * CAP
        wanted = lax.broadcasted_iota(jnp.int32, (size, rows), 0) + at * CAP
        pick = jnp.where(slot == wanted, 1.0, 0.0).astype(jnp.bfloat16)
        sums[n % 2][:size] = jnp.dot(pick, unit[...], preferred_element_type=jnp.float32)
        if n:
            finish(n - 1)
    finish(blocks - 1)
    for n in range(blocks):
        store(n).wait()
    keep_slots.wait()


def pack(embeddings, labels, row_ids, groups):
    rows, width = embeddings.shape
    lines = rows // LANES
    depth = width // LANES * CAP + 8
    parts, blocks = 1, len(PACK_ENDS)
    there = pl.BlockSpec(memory_space=pl.ANY)
    return pl.pallas_call(
        pack_kernel,
        in_specs=[there] * 3,
        out_specs=[there] * 2,
        out_shape=[
            jax.ShapeDtypeStruct((groups, depth, LANES), jnp.bfloat16),
            jax.ShapeDtypeStruct((1, rows), jnp.int32),
        ],
        scratch_shapes=[
            pltpu.VMEM((lines, LANES), jnp.int32),
            pltpu.VMEM((lines, LANES), jnp.int32),
            pltpu.VMEM((rows, width), jnp.bfloat16),
            pltpu.VMEM((rows, width), jnp.bfloat16),
            pltpu.VMEM((groups, depth, LANES), jnp.bfloat16),
            pltpu.VMEM((1, rows), jnp.int32),
            pltpu.VMEM((groups * 3 // 4 * CAP, width), jnp.float32),
            pltpu.VMEM((groups * 3 // 4 * CAP, width), jnp.float32),
            pltpu.SemaphoreType.DMA((parts,)),
            pltpu.SemaphoreType.DMA((blocks,)),
            pltpu.SemaphoreType.DMA((3,)),
        ],
        compiler_params=pltpu.CompilerParams(vmem_limit_bytes=62 << 20),
        cost_estimate=pl.CostEstimate(
            flops=2 * groups * CAP * rows * width, bytes_accessed=6 * rows * width, transcendentals=rows
        ),
    )(labels.reshape(lines, LANES), row_ids.reshape(lines, LANES), embeddings)


def codes(block):
    tags = block.astype(jnp.float32)[:, 0, :]
    second, third = pltpu.roll(tags, LANES - CAP, 1), pltpu.roll(tags, LANES - 2 * CAP, 1)
    return (third - 1.0) * 65536.0 + second * 256.0 + tags


def low_of(code):
    return jnp.floor(code * (1.0 / 131072.0)) * 131072.0


def code_lines(ref, order):
    senders, depth, _ = ref.shape
    tail = depth // CAP * CAP
    per = LANES // CAP
    lines = senders // per
    lane = lax.broadcasted_iota(jnp.int32, (lines, LANES), 1)
    order[...] = codes(ref[:, tail : tail + 8, :])
    code = order[pl.ds(0, lines, stride=per), :]
    for k in range(1, per):
        turned = pltpu.roll(order[pl.ds(k, lines, stride=per), :], k * CAP, 1)
        code = jnp.where(lane >= k * CAP, turned, code)
    return code


def code_columns(ref, col_code, col_low):
    senders, depth, _ = ref.shape
    tail = depth // CAP * CAP
    tall = codes(ref[:, tail : tail + 8, :])
    tall = jnp.concatenate([tall, jnp.zeros((LANES - senders, LANES), jnp.float32)], axis=0).T
    for s in range(senders):
        col = jnp.broadcast_to(tall[:CAP, s : s + 1], (CAP, LANES))
        col_code[s * CAP : (s + 1) * CAP, :] = col
        col_low[s * CAP : (s + 1) * CAP, :] = low_of(col)


def rows_of(ref, sender, count):
    chunks = ref.shape[1] // CAP
    return jnp.concatenate(
        [
            ref[pl.ds(sender, count), j * CAP : (j + 1) * CAP, :].reshape(count * CAP, LANES)
            for j in range(chunks)
        ],
        axis=1,
    )


def reduce_tile(score, wide, row0, col_code, col_low, col_best, lanes):
    size = score.shape[0]
    step = 64
    tops = [None] * (wide // LANES)
    for r in range(0, size, step):
        rows = slice(row0 + r, row0 + r + step)
        code, low = col_code[rows, :], col_low[rows, :]
        side = None
        for c, (lane_code, lane_low, _, _, both) in enumerate(lanes):
            here = score[r : r + step, c * LANES : (c + 1) * LANES]
            here = jnp.where(low == lane_low, here, -1.0)
            less = code < lane_code
            top = jnp.max(jnp.where(less, here, -1.0).reshape(step // 8, 8, LANES), axis=0)
            tops[c] = top if tops[c] is None else jnp.maximum(tops[c], top)
            if both:
                late = jnp.where(less, -1.0, here)
                side = late if side is None else jnp.maximum(side, late)
        if side is not None:
            col_best[rows, :] = jnp.maximum(col_best[rows, :], side)
    for top, (_, _, read, write, _) in zip(tops, lanes):
        write(jnp.maximum(read(), top))


def column_maxima(col_best, row0, size):
    return [
        jnp.max(col_best[t : t + LANES, :].T, axis=0, keepdims=True)
        for t in range(row0, row0 + size, LANES)
    ]


def own_kernel(own_ref, out_ref, col_code, col_low, order, lane_code, lane_low, col_best, best, *scores):
    senders = own_ref.shape[0]
    count = senders * CAP
    size, most = scores[0].shape

    def prepare():
        code = code_lines(own_ref, order)
        low = low_of(code)
        for t in range(count // LANES):
            lane_code[:, t * LANES : (t + 1) * LANES] = code[t : t + 1]
            lane_low[:, t * LANES : (t + 1) * LANES] = low[t : t + 1]
        code_columns(own_ref, col_code, col_low)
        col_best[...] = jnp.full(col_best.shape, -1.0, jnp.float32)
        best[...] = jnp.full(best.shape, -1.0, jnp.float32)

    def reduce(at, r0, c0, wide):
        lanes = []
        for c in range(c0, c0 + wide, LANES):
            span = slice(c, c + LANES)

            def read(span=span):
                return best[:, span]

            def write(x, span=span):
                best[:, span] = x

            lanes.append((lane_code[:, span], lane_low[:, span], read, write, c >= r0 + size))
        reduce_tile(scores[at], wide, r0, col_code, col_low, col_best, lanes)

    tiles = [
        (r0, c0, min(most, count - c0)) for r0 in range(0, count, size) for c0 in range(r0, count, most)
    ]
    tops = []
    for n in range(len(tiles) + 1):
        if n < len(tiles):
            r0, c0, wide = tiles[n]
            scores[n % 2][:, :wide] = lax.dot_general(
                rows_of(own_ref, r0 // CAP, size // CAP),
                rows_of(own_ref, c0 // CAP, wide // CAP),
                NT,
                preferred_element_type=jnp.float32,
            )
        if n == 0:
            prepare()
            continue
        r0, c0, wide = tiles[n - 1]
        reduce((n - 1) % 2, r0, c0, wide)
        if c0 + wide == count:
            tops += column_maxima(col_best, r0, size)
    top = jnp.max(best[...], axis=0, keepdims=True)
    top = jnp.concatenate([top[:, t : t + LANES] for t in range(0, count, LANES)], axis=0)
    out_ref[...] = jnp.maximum(top, jnp.concatenate(tops, axis=0))


def cross_kernel(
    own_ref, other_ref, prev_ref, col_code, col_low, out_ref, order, lane_code, lane_low, col_best, best, *scores
):
    senders = own_ref.shape[0]
    count = senders * CAP
    size, most = scores[0].shape
    blocks = count // size
    each = size // LANES
    core = lax.axis_index("blk")

    def prepare():
        code = code_lines(other_ref, order)
        low = low_of(code)
        for t in range(count // LANES):
            span = slice(t % each * LANES, (t % each + 1) * LANES)
            lane_code[t // each : t // each + 1, span] = code[t : t + 1]
            lane_low[t // each : t // each + 1, span] = low[t : t + 1]
        col_best[...] = jnp.full(col_best.shape, -1.0, jnp.float32)
        best[...] = jnp.full(best.shape, -1.0, jnp.float32)

    def reduce(at, n, others):
        lanes = []
        for j in others:
            code_here, low_here = lane_code[pl.ds(j, 1), :], lane_low[pl.ds(j, 1), :]
            for c in range(0, size, LANES):
                span = slice(c, c + LANES)

                def read(j=j, span=span):
                    return best[j, :, span]

                def write(x, j=j, span=span):
                    best[j, :, span] = x

                lanes.append((code_here[:, span], low_here[:, span], read, write, True))
        reduce_tile(scores[at], len(others) * size, n * size, col_code, col_low, col_best, lanes)

    tiles = [(n, [lax.rem(n + core + k, blocks) for k in range(blocks // 2)]) for n in range(blocks)]
    tiles = tiles[:-1] + [(blocks - 1, [j]) for j in tiles[-1][1]]
    tops = []
    for t in range(len(tiles) + 1):
        if t < len(tiles):
            n, others = tiles[t]
            scores[t % 2][:, : len(others) * size] = lax.dot_general(
                rows_of(own_ref, n * size // CAP, size // CAP),
                jnp.concatenate(
                    [rows_of(other_ref, j * (size // CAP), size // CAP) for j in others], axis=0
                ),
                NT,
                preferred_element_type=jnp.float32,
            )
        if t == 0:
            prepare()
            continue
        n, others = tiles[t - 1]
        reduce((t - 1) % 2, n, others)
        if t == len(tiles) or tiles[t][0] != n:
            tops += column_maxima(col_best, n * size, size)

    per = LANES // CAP
    lines = senders // per
    mine = jnp.maximum(prev_ref[...], jnp.concatenate(tops, axis=0))
    theirs = jnp.concatenate(
        [
            jnp.max(best[t // each, :, t % each * LANES : (t % each + 1) * LANES], axis=0, keepdims=True)
            for t in range(lines)
        ],
        axis=0,
    )
    lane = lax.broadcasted_iota(jnp.int32, (lines, LANES), 1)
    for k in range(per):
        first = pltpu.roll(mine, LANES - k * CAP, 1) if k else mine
        second = pltpu.roll(theirs, (LANES + CAP - k * CAP) % LANES, 1) if k != 1 else theirs
        order[pl.ds(k, lines, stride=per), :] = jnp.where(lane < CAP, first, second)
    out_ref[...] = order[...]


def gram_call(kernel, out_shapes, operands, blocked, senders, depth, pairs):
    count = senders * CAP
    size = min(512, count)
    most = min(1024, count)
    here = pl.BlockSpec(memory_space=pltpu.VMEM)
    lanes = (count // size, size) if blocked else (1, count)
    tops = (count // size, 8, size) if blocked else (8, count)
    return pl.pallas_call(
        kernel,
        in_specs=[here] * len(operands),
        out_specs=[here] * len(out_shapes),
        out_shape=[jax.ShapeDtypeStruct(shape, jnp.float32) for shape in out_shapes],
        scratch_shapes=[
            pltpu.VMEM((senders, LANES), jnp.float32),
            pltpu.VMEM(lanes, jnp.float32),
            pltpu.VMEM(lanes, jnp.float32),
            pltpu.VMEM((count, LANES), jnp.float32),
            pltpu.VMEM(tops, jnp.float32),
            pltpu.VMEM((size, most), jnp.float32),
            pltpu.VMEM((size, most), jnp.float32),
        ],
        compiler_params=pltpu.CompilerParams(vmem_limit_bytes=24 << 20),
        cost_estimate=pl.CostEstimate(
            flops=2 * pairs * (depth // CAP) * LANES,
            bytes_accessed=4 * count * (depth // CAP) * LANES,
            transcendentals=0,
        ),
    )(*operands)


def unpack_kernel(back_ref, swap_ref, slot_ref, out_ref):
    groups = back_ref.shape[0]
    rows = slot_ref.shape[1]
    slot = slot_ref[...]
    group = lax.shift_right_logical(slot, 5)
    rank = slot & (CAP - 1)
    member = lax.broadcasted_iota(jnp.int32, (groups, rows), 0) == group
    member = jnp.where(member, 1.0, 0.0).astype(jnp.bfloat16)
    rest = jnp.maximum(back_ref[...], pltpu.roll(swap_ref[...], LANES - CAP, 1))[:, :CAP]
    found = jnp.zeros((CAP, rows), jnp.float32)
    for _ in range(3):
        piece = rest.astype(jnp.bfloat16)
        rest = rest - piece.astype(jnp.float32)
        found += lax.dot_general(
            piece, member, (((0,), (0,)), ((), ())), preferred_element_type=jnp.float32
        )
    chosen = lax.broadcasted_iota(jnp.int32, (CAP, rows), 0) == rank
    best = jnp.sum(jnp.where(chosen, found, 0.0), axis=0, keepdims=True)
    out_ref[...] = jnp.concatenate(
        [best[:, b * LANES : (b + 1) * LANES] for b in range(rows // LANES)], axis=0
    )


def unpack(back, swap, slot):
    rows = slot.shape[1]
    return pl.pallas_call(
        unpack_kernel,
        out_shape=jax.ShapeDtypeStruct((rows // LANES, LANES), jnp.float32),
        compiler_params=pltpu.CompilerParams(vmem_limit_bytes=16 << 20),
    )(back, swap, slot)


def local(embeddings, labels, row_ids):
    groups = lax.axis_size("grp")
    rows = embeddings.shape[0]
    send, slot = pack(embeddings, labels, row_ids, groups)
    own = lax.all_to_all(send, "grp", split_axis=0, concat_axis=0, tiled=True)
    swap = [(0, 1), (1, 0)]
    other = lax.ppermute(own, "blk", swap)
    depth = own.shape[1]
    count = groups * CAP
    found, col_code, col_low = gram_call(
        own_kernel,
        [(count // LANES, LANES), (count, LANES), (count, LANES)],
        [own],
        False,
        groups,
        depth,
        count * count * 5 // 8,
    )
    [found] = gram_call(
        cross_kernel,
        [(groups, LANES)],
        [own, other, found, col_code, col_low],
        True,
        groups,
        depth,
        count * count // 2,
    )
    back = lax.all_to_all(found, "grp", split_axis=0, concat_axis=0, tiled=True)
    return unpack(back, lax.ppermute(back, "blk", swap), slot).reshape(rows)


def solution(mesh):
    in_specs = (P(("grp", "blk"), None), P(("grp", "blk")), P(("grp", "blk")))
    out_specs = P(("grp", "blk"))
    return jax.shard_map(local, mesh=mesh, in_specs=in_specs, out_specs=out_specs, check_vma=False)
```

```python
import functools

import jax
import jax.numpy as jnp
from jax import lax
from jax.experimental import pallas as pl
from jax.experimental.pallas import tpu as pltpu
from jax.sharding import PartitionSpec as P

CAP = 32
CL_GRP = 16
LANES = 128
PACK_ENDS = (8, 13, 15, 16)
NT = (((1,), (1,)), ((), ()))


def pack_kernel(
    labels_ref, ids_ref, emb_ref, out_ref, slot_ref, lab, num, raw, unit, stage, slots, first, second, in_sems, out_sems, sems
):
    rows, width = unit.shape
    groups = out_ref.shape[0]
    lines = rows // LANES
    parts, blocks = in_sems.shape[0], out_sems.shape[0]
    part = rows // parts
    ends = [groups * n // 16 for n in PACK_ENDS]
    spans = list(zip([0] + ends[:-1], ends))
    fetch_labels = pltpu.make_async_copy(labels_ref, lab, sems.at[0])
    fetch_ids = pltpu.make_async_copy(ids_ref, num, sems.at[1])
    keep_slots = pltpu.make_async_copy(slots, slot_ref, sems.at[2])
    tail = width // LANES * CAP

    def load(p):
        span = pl.ds(p * part, part)
        return pltpu.make_async_copy(emb_ref.at[span], raw.at[span], in_sems.at[p])

    def store(n):
        span = pl.ds(spans[n][0], spans[n][1] - spans[n][0])
        return pltpu.make_async_copy(stage.at[span], out_ref.at[span], out_sems.at[n])

    fetch_labels.start()
    fetch_ids.start()
    for p in range(parts):
        load(p).start()

    fetch_labels.wait()
    fetch_ids.wait()
    labels = lab[...]
    place = (
        lax.broadcasted_iota(jnp.int32, (lines, LANES), 0) * LANES
        + lax.broadcasted_iota(jnp.int32, (lines, LANES), 1)
    )
    key = (labels * rows + place).astype(jnp.float32)
    target = lax.shift_right_logical(labels, 4)
    low = (target * (CL_GRP * rows)).astype(jnp.float32)
    tall = jnp.concatenate([key, jnp.zeros((LANES - lines, LANES), jnp.float32)], axis=0).T

    def flat(x):
        return jnp.concatenate([x[b : b + 1] for b in range(lines)], axis=1)

    key_row, low_row = flat(key), flat(low)
    count = jnp.zeros((LANES, rows), jnp.float32)
    for b in range(lines):
        col = tall[:, b : b + 1]
        count += jnp.where((col >= low_row) & (col < key_row), 1.0, 0.0)
    rank = jnp.sum(count, axis=0, keepdims=True).astype(jnp.int32)
    group = flat(target)
    slot = group * CAP + rank
    slots[...] = slot

    ids = num[...]
    pieces = [
        ids & 255,
        lax.shift_right_logical(ids, 8) & 255,
        (labels & (CL_GRP - 1)) * 2 + lax.shift_right_logical(ids, 16) + 1,
    ]
    ranked = lax.broadcasted_iota(jnp.int32, (CAP, rows), 0) == rank
    tags = [jnp.where(ranked, flat(x).astype(jnp.float32), 0.0) for x in pieces]
    tags.append(jnp.zeros((LANES - CAP * len(pieces), rows), jnp.float32))
    tags = jnp.concatenate(tags, axis=0).astype(jnp.bfloat16)
    member = lax.broadcasted_iota(jnp.int32, (LANES, rows), 0) == group
    member = jnp.where(member, 1.0, 0.0).astype(jnp.bfloat16)
    tags = lax.dot_general(member, tags, NT, preferred_element_type=jnp.float32)[:groups]
    stage[:, tail : tail + 8, :] = jnp.broadcast_to(
        tags.reshape(groups, 1, LANES), (groups, 8, LANES)
    ).astype(jnp.bfloat16)

    for p in range(parts):
        load(p).wait()
        wide = raw[p * part : (p + 1) * part].astype(jnp.float32)
        scale = lax.rsqrt(jnp.sum(wide * wide, axis=1, keepdims=True) + 1e-06)
        unit[p * part : (p + 1) * part] = (wide * scale).astype(jnp.bfloat16)

    sums = (first, second)

    def finish(n):
        at, end = spans[n]
        packed = sums[n % 2][: (end - at) * CAP].astype(jnp.bfloat16)
        for j in range(width // LANES):
            stage[at:end, j * CAP : (j + 1) * CAP, :] = packed[
                :, j * LANES : (j + 1) * LANES
            ].reshape(end - at, CAP, LANES)
        store(n).start()
        if n == 0:
            keep_slots.start()

    for n, (at, end) in enumerate(spans):
        size = (end - at) * CAP
        wanted = lax.broadcasted_iota(jnp.int32, (size, rows), 0) + at * CAP
        pick = jnp.where(slot == wanted, 1.0, 0.0).astype(jnp.bfloat16)
        sums[n % 2][:size] = jnp.dot(pick, unit[...], preferred_element_type=jnp.float32)
        if n:
            finish(n - 1)
    finish(blocks - 1)
    for n in range(blocks):
        store(n).wait()
    keep_slots.wait()


def pack(embeddings, labels, row_ids, groups):
    rows, width = embeddings.shape
    lines = rows // LANES
    depth = width // LANES * CAP + 8
    parts, blocks = 1, len(PACK_ENDS)
    there = pl.BlockSpec(memory_space=pl.ANY)
    return pl.pallas_call(
        pack_kernel,
        in_specs=[there] * 3,
        out_specs=[there] * 2,
        out_shape=[
            jax.ShapeDtypeStruct((groups, depth, LANES), jnp.bfloat16),
            jax.ShapeDtypeStruct((1, rows), jnp.int32),
        ],
        scratch_shapes=[
            pltpu.VMEM((lines, LANES), jnp.int32),
            pltpu.VMEM((lines, LANES), jnp.int32),
            pltpu.VMEM((rows, width), jnp.bfloat16),
            pltpu.VMEM((rows, width), jnp.bfloat16),
            pltpu.VMEM((groups, depth, LANES), jnp.bfloat16),
            pltpu.VMEM((1, rows), jnp.int32),
            pltpu.VMEM((groups * 3 // 4 * CAP, width), jnp.float32),
            pltpu.VMEM((groups * 3 // 4 * CAP, width), jnp.float32),
            pltpu.SemaphoreType.DMA((parts,)),
            pltpu.SemaphoreType.DMA((blocks,)),
            pltpu.SemaphoreType.DMA((3,)),
        ],
        compiler_params=pltpu.CompilerParams(vmem_limit_bytes=62 << 20),
        cost_estimate=pl.CostEstimate(
            flops=2 * groups * CAP * rows * width, bytes_accessed=6 * rows * width, transcendentals=rows
        ),
    )(labels.reshape(lines, LANES), row_ids.reshape(lines, LANES), embeddings)


def codes(block):
    tags = block.astype(jnp.float32)[:, 0, :]
    second, third = pltpu.roll(tags, LANES - CAP, 1), pltpu.roll(tags, LANES - 2 * CAP, 1)
    return (third - 1.0) * 65536.0 + second * 256.0 + tags


def low_of(code):
    return jnp.floor(code * (1.0 / 131072.0)) * 131072.0


def code_lines(ref, order):
    senders, depth, _ = ref.shape
    tail = depth // CAP * CAP
    per = LANES // CAP
    lines = senders // per
    lane = lax.broadcasted_iota(jnp.int32, (lines, LANES), 1)
    order[...] = codes(ref[:, tail : tail + 8, :])
    code = order[pl.ds(0, lines, stride=per), :]
    for k in range(1, per):
        turned = pltpu.roll(order[pl.ds(k, lines, stride=per), :], k * CAP, 1)
        code = jnp.where(lane >= k * CAP, turned, code)
    return code


def code_columns(ref, col_code, col_low):
    senders, depth, _ = ref.shape
    tail = depth // CAP * CAP
    tall = codes(ref[:, tail : tail + 8, :])
    tall = jnp.concatenate([tall, jnp.zeros((LANES - senders, LANES), jnp.float32)], axis=0).T
    for s in range(senders):
        col = jnp.broadcast_to(tall[:CAP, s : s + 1], (CAP, LANES))
        col_code[s * CAP : (s + 1) * CAP, :] = col
        col_low[s * CAP : (s + 1) * CAP, :] = low_of(col)


def rows_of(ref, sender, count):
    chunks = ref.shape[1] // CAP
    return jnp.concatenate(
        [
            ref[pl.ds(sender, count), j * CAP : (j + 1) * CAP, :].reshape(count * CAP, LANES)
            for j in range(chunks)
        ],
        axis=1,
    )


def reduce_tile(score, wide, row0, col_code, col_low, col_best, lanes):
    size = score.shape[0]
    step = 64
    tops = [None] * (wide // LANES)
    for r in range(0, size, step):
        rows = slice(row0 + r, row0 + r + step)
        code, low = col_code[rows, :], col_low[rows, :]
        side = None
        for c, (lane_code, lane_low, _, _, both) in enumerate(lanes):
            here = score[r : r + step, c * LANES : (c + 1) * LANES]
            here = jnp.where(low == lane_low, here, -1.0)
            less = code < lane_code
            top = jnp.max(jnp.where(less, here, -1.0).reshape(step // 8, 8, LANES), axis=0)
            tops[c] = top if tops[c] is None else jnp.maximum(tops[c], top)
            if both:
                late = jnp.where(less, -1.0, here)
                side = late if side is None else jnp.maximum(side, late)
        if side is not None:
            col_best[rows, :] = jnp.maximum(col_best[rows, :], side)
    for top, (_, _, read, write, _) in zip(tops, lanes):
        write(jnp.maximum(read(), top))


def column_maxima(col_best, row0, size):
    return [
        jnp.max(col_best[t : t + LANES, :].T, axis=0, keepdims=True)
        for t in range(row0, row0 + size, LANES)
    ]


def own_kernel(own_ref, out_ref, col_code, col_low, order, lane_code, lane_low, col_best, best, *scores):
    senders = own_ref.shape[0]
    count = senders * CAP
    size, most = scores[0].shape

    def prepare():
        code = code_lines(own_ref, order)
        low = low_of(code)
        for t in range(count // LANES):
            lane_code[:, t * LANES : (t + 1) * LANES] = code[t : t + 1]
            lane_low[:, t * LANES : (t + 1) * LANES] = low[t : t + 1]
        code_columns(own_ref, col_code, col_low)
        col_best[...] = jnp.full(col_best.shape, -1.0, jnp.float32)
        best[...] = jnp.full(best.shape, -1.0, jnp.float32)

    def reduce(at, r0, c0, wide):
        lanes = []
        for c in range(c0, c0 + wide, LANES):
            span = slice(c, c + LANES)

            def read(span=span):
                return best[:, span]

            def write(x, span=span):
                best[:, span] = x

            lanes.append((lane_code[:, span], lane_low[:, span], read, write, c >= r0 + size))
        reduce_tile(scores[at], wide, r0, col_code, col_low, col_best, lanes)

    tiles = [
        (r0, c0, min(most, count - c0)) for r0 in range(0, count, size) for c0 in range(r0, count, most)
    ]
    tops = []
    for n in range(len(tiles) + 1):
        if n < len(tiles):
            r0, c0, wide = tiles[n]
            scores[n % 2][:, :wide] = lax.dot_general(
                rows_of(own_ref, r0 // CAP, size // CAP),
                rows_of(own_ref, c0 // CAP, wide // CAP),
                NT,
                preferred_element_type=jnp.float32,
            )
        if n == 0:
            prepare()
            continue
        r0, c0, wide = tiles[n - 1]
        reduce((n - 1) % 2, r0, c0, wide)
        if c0 + wide == count:
            tops += column_maxima(col_best, r0, size)
    top = jnp.max(best[...], axis=0, keepdims=True)
    top = jnp.concatenate([top[:, t : t + LANES] for t in range(0, count, LANES)], axis=0)
    out_ref[...] = jnp.maximum(top, jnp.concatenate(tops, axis=0))


def cross_kernel(
    own_ref, other_ref, prev_ref, col_code, col_low, out_ref, order, lane_code, lane_low, col_best, best, *scores
):
    senders = own_ref.shape[0]
    count = senders * CAP
    size, most = scores[0].shape
    blocks = count // size
    each = size // LANES
    core = lax.axis_index("blk")

    def prepare():
        code = code_lines(other_ref, order)
        low = low_of(code)
        for t in range(count // LANES):
            span = slice(t % each * LANES, (t % each + 1) * LANES)
            lane_code[t // each : t // each + 1, span] = code[t : t + 1]
            lane_low[t // each : t // each + 1, span] = low[t : t + 1]
        col_best[...] = jnp.full(col_best.shape, -1.0, jnp.float32)
        best[...] = jnp.full(best.shape, -1.0, jnp.float32)

    def reduce(at, row0, rows, others):
        lanes = []
        for j in others:
            code_here, low_here = lane_code[pl.ds(j, 1), :], lane_low[pl.ds(j, 1), :]
            for c in range(0, size, LANES):
                span = slice(c, c + LANES)

                def read(j=j, span=span):
                    return best[j, :, span]

                def write(x, j=j, span=span):
                    best[j, :, span] = x

                lanes.append((code_here[:, span], low_here[:, span], read, write, True))
        reduce_tile(scores[at].at[:rows], len(others) * size, row0, col_code, col_low, col_best, lanes)

    half = blocks // 2
    tiles = []
    for n in range(half):
        j = lax.rem(n + core, half)
        cut = [size, size] if n < half - 1 else [size, size // 2, size // 2]
        at = n * 2 * size
        for rows in cut:
            tiles.append((at, rows, j))
            at += rows
    tops = []
    for t in range(len(tiles) + 1):
        if t < len(tiles):
            at, rows, j = tiles[t]
            scores[t % 2][:rows] = lax.dot_general(
                rows_of(own_ref, at // CAP, rows // CAP),
                rows_of(other_ref, j * (2 * size // CAP), 2 * size // CAP),
                NT,
                preferred_element_type=jnp.float32,
            )
        if t == 0:
            prepare()
            continue
        at, rows, j = tiles[t - 1]
        reduce((t - 1) % 2, at, rows, [j * 2, j * 2 + 1])
        tops += column_maxima(col_best, at, rows)

    per = LANES // CAP
    lines = senders // per
    mine = jnp.maximum(prev_ref[...], jnp.concatenate(tops, axis=0))
    theirs = jnp.concatenate(
        [
            jnp.max(best[t // each, :, t % each * LANES : (t % each + 1) * LANES], axis=0, keepdims=True)
            for t in range(lines)
        ],
        axis=0,
    )
    lane = lax.broadcasted_iota(jnp.int32, (lines, LANES), 1)
    for k in range(per):
        first = pltpu.roll(mine, LANES - k * CAP, 1) if k else mine
        second = pltpu.roll(theirs, (LANES + CAP - k * CAP) % LANES, 1) if k != 1 else theirs
        order[pl.ds(k, lines, stride=per), :] = jnp.where(lane < CAP, first, second)
    out_ref[...] = order[...]


def gram_call(kernel, out_shapes, operands, blocked, senders, depth, pairs):
    count = senders * CAP
    size = min(512, count)
    most = min(1024, count)
    here = pl.BlockSpec(memory_space=pltpu.VMEM)
    lanes = (count // size, size) if blocked else (1, count)
    tops = (count // size, 8, size) if blocked else (8, count)
    return pl.pallas_call(
        kernel,
        in_specs=[here] * len(operands),
        out_specs=[here] * len(out_shapes),
        out_shape=[jax.ShapeDtypeStruct(shape, jnp.float32) for shape in out_shapes],
        scratch_shapes=[
            pltpu.VMEM((senders, LANES), jnp.float32),
            pltpu.VMEM(lanes, jnp.float32),
            pltpu.VMEM(lanes, jnp.float32),
            pltpu.VMEM((count, LANES), jnp.float32),
            pltpu.VMEM(tops, jnp.float32),
            pltpu.VMEM((size, most), jnp.float32),
            pltpu.VMEM((size, most), jnp.float32),
        ],
        compiler_params=pltpu.CompilerParams(vmem_limit_bytes=24 << 20),
        cost_estimate=pl.CostEstimate(
            flops=2 * pairs * (depth // CAP) * LANES,
            bytes_accessed=4 * count * (depth // CAP) * LANES,
            transcendentals=0,
        ),
    )(*operands)


def unpack_kernel(back_ref, swap_ref, slot_ref, out_ref):
    groups = back_ref.shape[0]
    rows = slot_ref.shape[1]
    slot = slot_ref[...]
    group = lax.shift_right_logical(slot, 5)
    rank = slot & (CAP - 1)
    member = lax.broadcasted_iota(jnp.int32, (groups, rows), 0) == group
    member = jnp.where(member, 1.0, 0.0).astype(jnp.bfloat16)
    rest = jnp.maximum(back_ref[...], pltpu.roll(swap_ref[...], LANES - CAP, 1))[:, :CAP]
    found = jnp.zeros((CAP, rows), jnp.float32)
    for _ in range(3):
        piece = rest.astype(jnp.bfloat16)
        rest = rest - piece.astype(jnp.float32)
        found += lax.dot_general(
            piece, member, (((0,), (0,)), ((), ())), preferred_element_type=jnp.float32
        )
    chosen = lax.broadcasted_iota(jnp.int32, (CAP, rows), 0) == rank
    best = jnp.sum(jnp.where(chosen, found, 0.0), axis=0, keepdims=True)
    out_ref[...] = jnp.concatenate(
        [best[:, b * LANES : (b + 1) * LANES] for b in range(rows // LANES)], axis=0
    )


def unpack(back, swap, slot):
    rows = slot.shape[1]
    return pl.pallas_call(
        unpack_kernel,
        out_shape=jax.ShapeDtypeStruct((rows // LANES, LANES), jnp.float32),
        compiler_params=pltpu.CompilerParams(vmem_limit_bytes=16 << 20),
    )(back, swap, slot)


def local(embeddings, labels, row_ids):
    groups = lax.axis_size("grp")
    rows = embeddings.shape[0]
    send, slot = pack(embeddings, labels, row_ids, groups)
    own = lax.all_to_all(send, "grp", split_axis=0, concat_axis=0, tiled=True)
    swap = [(0, 1), (1, 0)]
    other = lax.ppermute(own, "blk", swap)
    depth = own.shape[1]
    count = groups * CAP
    found, col_code, col_low = gram_call(
        own_kernel,
        [(count // LANES, LANES), (count, LANES), (count, LANES)],
        [own],
        False,
        groups,
        depth,
        count * count * 5 // 8,
    )
    [found] = gram_call(
        cross_kernel,
        [(groups, LANES)],
        [own, other, found, col_code, col_low],
        True,
        groups,
        depth,
        count * count // 2,
    )
    back = lax.all_to_all(found, "grp", split_axis=0, concat_axis=0, tiled=True)
    return unpack(back, lax.ppermute(back, "blk", swap), slot).reshape(rows)


def solution(mesh):
    in_specs = (P(("grp", "blk"), None), P(("grp", "blk")), P(("grp", "blk")))
    out_specs = P(("grp", "blk"))
    return jax.shard_map(local, mesh=mesh, in_specs=in_specs, out_specs=out_specs, check_vma=False)
```
